32 devices in a mesh: comp: 2 (over y), ty: 4 (over z), tx: 4 (over x, core).
Axes of the slice: x: 2, y: 2, z: 4, core: 2. Of those that a mesh axis runs over, the one named last changes fastest.
Arguments:
- atm_flux: float32 [8, 524288], P(None, ('comp', 'ty', 'tx')), may hold values from -6 to 6
- margin_source: int32 [8192, 128], P(('comp', 'ty', 'tx')), may hold values from 0 to 127
- margin_cell: int32 [8192, 128], P(('comp', 'ty', 'tx')), may hold values from 0 to 65535, as said below
- margin_weight: float32 [8192, 128], P(('comp', 'ty', 'tx')), may hold values from 0 to 1
- margin_tile: int32 [8192, 1], P(('comp', 'ty', 'tx')), may hold values from 0 to 31; in each aligned block of 256 rows (0 to 255, 256 to 511, ...) at most 16 rows name the same one
- land_mask: int32 [512, 4096], P(('comp', 'ty'), 'tx'), may hold values 0 or 1
- sea_depth: float32 [512, 4096], P(('comp', 'ty'), 'tx'), may hold values from 0.5 to 1.8
- sea_height: float32 [512, 4096], P(('comp', 'ty'), 'tx'), may hold values from -3 to 3
- transport: float32 [2, 512, 4096], P(None, ('comp', 'ty'), 'tx'), may hold values from -3 to 3
- tracers: float32 [2, 16, 512, 4096], P(None, None, ('comp', 'ty'), 'tx'), may hold values from -6 to 6
Outputs:
- new_height: float32 [512, 4096], P(('comp', 'ty'), 'tx')
- new_transport: float32 [2, 512, 4096], P(None, ('comp', 'ty'), 'tx')
- new_tracers: float32 [2, 16, 512, 4096], P(None, None, ('comp', 'ty'), 'tx')
The draws below stay inside these ranges and needn't reach their ends.
Inputs may be any that keep to these rules, and one draw needn't show every extreme that they name: `margin_tile`: among the 256 blocks of one atmosphere owner (an aligned run of 256 rows), no ocean tile is named by more than 16 blocks. All entries of one block lie in one row of its tile: margin_cell[b, j] // 1024 is the same for every j.
All inputs are finite; a program needn't handle non-finite values. No bound on the sum of `land_mask` on one device may be relied on, other than what follows from the above.
Results may differ from the reference program's by a relative error of at most 0.000088.
Values sent between devices are 32-bit elements; how exact they have to be, the bound alone decides.
A program may use at most 192 MiB of HBM per device.

```python
import math
import jax
import jax.numpy as jnp
import numpy as np
from jax import lax

NFLUX = 8
LEV = 16
SUB = 3
BW = 128
CY = 64
CX = 1024
BLK_DEV = 256
ACOL_DEV = 16384
CAP = 16
TCOLS = 4
NY = 512
NX = 4096
NBT = 8192
ACOLS = 524288
DEVICES = 32


def draw_margin_cell(key, part):
    row_key = jax.random.fold_in(key, 11)
    col_key = jax.random.fold_in(key, 12)
    rows = jax.random.randint(row_key, (NBT, 1), 0, CY)
    cols = jax.random.randint(col_key, (NBT, BW), 0, CX)
    return (rows * CX + cols).astype(jnp.int32)


def place_ends(values, own_key, low, largest):
    index_at = [jax.random.randint(jax.random.fold_in(own_key, axis), (), 0, length) for axis, length in enumerate(values.shape)]
    main_axis = values.shape.index(max(values.shape))
    beside = index_at[:main_axis] + [(index_at[main_axis] + 1) % values.shape[main_axis]] + index_at[main_axis + 1:]
    return values.at[tuple(index_at)].set(low).at[tuple(beside)].set(largest)


def block_scale(stream_key, dims, split, least, top_value):
    gain, own = 1.0, jax.random.fold_in(stream_key, 6)
    for dim, parts in split:
        draws = jnp.exp(jax.random.uniform(jax.random.fold_in(own, dim), (parts,), jnp.float32, least / len(split), top_value / len(split)))
        gain = gain * jnp.repeat(draws, dims[dim] // parts).reshape([-1 if axis == dim else 1 for axis in range(len(dims))])
    return gain


def deal_out(rng, own, number, rows, number_of, top, limit, lean):
    ranking = jax.random.permutation(rng, number_of)
    crowded, usual = shares(number_of, rows * top, limit, lean, True), shares(number_of, rows * top, limit, lean, False)
    places = jnp.arange(number_of)

    def named(tallies, offset_by):
        used = int((tallies > 0).sum())
        fixed = max(1, used // 4)
        passed = fixed + (places - fixed + offset_by * (used - fixed)) % max(1, number_of - fixed)
        return jnp.zeros((number_of,), jnp.int32).at[ranking[jnp.where(places < fixed, places, passed)]].set(jnp.asarray(tallies, jnp.int32))

    tallies = jnp.where(number % 4 == 0, named(crowded, number // 4), named(usual, number - number // 4 - 1))
    mixed = jax.random.permutation(jax.random.fold_in(own, 3), number_of)
    donor, taker = mixed[0:number_of // 2 * 2:2], mixed[1:number_of // 2 * 2:2]
    margin = jnp.minimum(tallies[donor] - 1, limit - tallies[taker]) // 2
    margin = jnp.where((donor == ranking[0]) | (taker == ranking[0]) | (tallies[taker] == 0), 0, jnp.maximum(margin, 0))
    passed = jax.random.randint(jax.random.fold_in(own, 4), (number_of // 2,), 0, 1 << 20) % (margin + 1)
    tallies = tallies.at[donor].add(-passed).at[taker].add(passed)
    labels = jnp.searchsorted(jnp.cumsum(tallies), jnp.arange(rows * top), side="right").astype(jnp.int32)
    table = labels.reshape(top, rows).T
    table = table[jax.random.permutation(jax.random.fold_in(own, 1), rows)]
    offset_by = jax.random.randint(jax.random.fold_in(own, 2), (rows, 1), 0, top)
    return jnp.take_along_axis(table, (jnp.arange(top)[None, :] + offset_by) % top, axis=1)


def shares(count, total, bound, slope, full):
    loads = [(1 << 20) // math.isqrt(rank ** slope) + 1 for rank in range(1, count + 1)]
    largest = bound if full else min(bound, max(-(-total // count), total * loads[0] // sum(loads)))
    least = 1 if total - largest >= count - 1 else 0
    holding, rest = [largest] + [least] * (count - 1), total - largest - least * (count - 1)
    while rest > 0:
        candidates = [i for i in range(1, count) if holding[i] < largest] or [i for i in range(1, count) if holding[i] < bound]
        mass, budget = sum([loads[i] for i in candidates]), rest
        for i in candidates:
            more = min(bound - holding[i], max(1, budget * loads[i] // mass), rest)
            holding[i] = holding[i] + more
            rest = rest - more
    return np.array(holding)


def scatter_about(rng, dims, scale, reach, cuts=(), held_as=jnp.bfloat16):
    entries = jax.random.normal(rng, dims, jnp.float32) * scale
    if len(cuts) > 0:
        entries = block_scale(rng, dims, cuts, -0.22, 0.18) * entries
    return jnp.clip(entries, min=-reach, max=reach).astype(held_as)


def setup_inputs(seed: int = 0) -> dict:
    splits = jax.random.split(jax.random.key(seed), 11)
    atm_flux = scatter_about(splits[0], (NFLUX, ACOLS), 1.0, 6.0, ((1, 32),), jnp.float32)
    margin_source = place_ends(jax.random.randint(splits[1], (NBT, BW), 0, BW), jax.random.fold_in(splits[1], 1), 0, BW - 1).astype(jnp.int32)
    margin_cell = draw_margin_cell(jax.random.fold_in(splits[10], 71), 0)
    margin_weight = jnp.clip(1.0 * jax.random.uniform(splits[3], (NBT, BW), jnp.float32) ** block_scale(splits[3], (NBT, BW), ((0, 32),), -0.2, 0.2), 0.0, 1.0)
    margin_tile_keys = jax.random.split(jax.random.fold_in(splits[4], 1), NBT // BLK_DEV)
    margin_tile_turns = jax.random.permutation(jax.random.fold_in(splits[4], 3), NBT // BLK_DEV)
    margin_tile = jax.vmap(lambda own, number: deal_out(jax.random.fold_in(splits[4], 2), own, number, BLK_DEV, DEVICES, 1, CAP, 2))(margin_tile_keys, margin_tile_turns).reshape((NBT, 1))
    land_mask = place_ends((jax.random.randint(splits[5], (NY, NX), 0, 4) < 3).astype(jnp.int32), jax.random.fold_in(splits[5], 1), 0, 1)
    sea_depth = jnp.clip(jnp.exp(math.log(1.8) - 1.2809338 * jax.random.uniform(splits[6], (NY, NX), jnp.float32) ** block_scale(splits[6], (NY, NX), ((0, 8), (1, 4)), -0.2, 0.2)), 0.5, 1.8)
    sea_height = scatter_about(splits[7], (NY, NX), 0.5, 3.0, ((0, 8), (1, 4)), jnp.float32)
    transport = scatter_about(splits[8], (2, NY, NX), 0.5, 3.0, ((1, 8), (2, 4)), jnp.float32)
    tracers = scatter_about(splits[9], (2, LEV, NY, NX), 1.0, 6.0, ((2, 8), (3, 4)), jnp.float32)
    return dict(atm_flux=atm_flux, margin_source=margin_source, margin_cell=margin_cell, margin_weight=margin_weight, margin_tile=margin_tile, land_mask=land_mask, sea_depth=sea_depth, sea_height=sea_height, transport=transport, tracers=tracers)


damping = 0.95
advect = 0.15
diffuse = 0.1


def four_sides(padded):
    eastern = padded[..., 1:-1, 2:]
    western = padded[..., 1:-1, :-2]
    northern = padded[..., 2:, 1:-1]
    southern = padded[..., :-2, 1:-1]
    return eastern, western, northern, southern


def zero_sides(values):
    padding = [(0, 0)] * (values.ndim - 2) + [(1, 1), (1, 1)]
    return four_sides(jnp.pad(values, padding))


def momentum(pressure_sides, along_flow, across, ocean_mask, bottom, wind_x, wind_y):
    eastern, western, northern, southern = pressure_sides
    along_flow = ocean_mask * (damping * along_flow + (-0.5 * bottom * (eastern - western) + wind_x))
    across = ocean_mask * (damping * across + (-0.5 * bottom * (northern - southern) + wind_y))
    return along_flow, across


def continuity(height, along_sides, across_sides, ocean_mask, source):
    divergence = along_sides[0] - along_sides[1] + across_sides[2] - across_sides[3]
    return ocean_mask * (height - 0.5 * divergence + source)


def barotropic(height, along_flow, across, ocean_mask, bottom, pressure_term, wind_x, wind_y, source, count):
    for k in range(count):
        pressure = ocean_mask * (height + pressure_term)
        along_flow, across = momentum(zero_sides(pressure), along_flow, across, ocean_mask, bottom, wind_x, wind_y)
        height = continuity(height, zero_sides(along_flow), zero_sides(across), ocean_mask, source)
    return height, along_flow, across


def horizontal(tracer_sides, mask_sides, tracers, transport, bottom):
    eastern, western, northern, southern = [
        edge_mask * near_value + (1.0 - edge_mask) * tracers
        for near_value, edge_mask in zip(tracer_sides, mask_sides)]
    east_speed = transport[0] / bottom
    north_speed = transport[1] / bottom
    carried = (jnp.maximum(east_speed, 0.0) * (tracers - western)
               + jnp.minimum(east_speed, 0.0) * (eastern - tracers)
               + jnp.maximum(north_speed, 0.0) * (tracers - southern)
               + jnp.minimum(north_speed, 0.0) * (northern - tracers))
    spread = eastern + western + northern + southern - 4.0 * tracers
    return tracers - advect * carried + diffuse * spread


def column_solve(heated, mixing):
    levels = heated.shape[1]
    nothing = jnp.zeros_like(mixing[0])
    ratios = []
    values = []
    last_ratio = nothing
    last_value = heated[:, 0]
    for k in range(levels):
        upper_mix = mixing[k] if k < levels - 1 else nothing
        lower_mix = mixing[k - 1] if k > 0 else nothing
        pivot_term = 1.0 + upper_mix + lower_mix
        right_side = heated[:, k]
        if k > 0:
            pivot_term = pivot_term + lower_mix * last_ratio
            right_side = right_side + lower_mix * last_value
        last_ratio = -upper_mix / pivot_term
        last_value = right_side / pivot_term
        ratios.append(last_ratio)
        values.append(last_value)
    result = [values[levels - 1]]
    for k in range(levels - 2, -1, -1):
        result.append(values[k] - ratios[k] * result[-1])
    return jnp.stack(result[::-1], axis=1)


def surface_and_mixing(moved, forcing):
    levels = moved.shape[1]
    depths = jnp.arange(levels, dtype=jnp.float32)
    absorb = jnp.exp(-depths / 3.0) - jnp.exp(-(depths + 1.0) / 3.0)
    heat = 0.5 * forcing[4][None] * absorb[:, None, None]
    heat = heat.at[0].add(0.5 * forcing[3])
    salt = jnp.zeros_like(heat).at[0].set(0.5 * forcing[5] - 0.3 * forcing[6])
    heated = moved + jnp.stack([heat, salt])
    mixing = 0.2 + 0.5 * (forcing[7] * forcing[7])[None] * jnp.exp(-depths[:-1] / 2.0)[:, None, None]
    return column_solve(heated, mixing)


def remap_fluxes(atm_flux, margin_source, margin_cell, margin_weight, margin_tile):
    block_ids = jnp.arange(margin_source.shape[0], dtype=jnp.int32)
    owner_device = block_ids // BLK_DEV
    window_start = ((block_ids % BLK_DEV) // 2) * BW
    columns = (owner_device * ACOL_DEV + window_start)[:, None] + margin_source
    target_tile = margin_tile[:, 0]
    row_index = (target_tile // TCOLS)[:, None] * CY + margin_cell // CX
    col_index = (target_tile % TCOLS)[:, None] * CX + margin_cell % CX
    places = (row_index * NX + col_index).reshape(-1)

    def spread_field(values):
        weighted = (values[columns] * margin_weight).reshape(-1)
        return jnp.zeros((NY * NX,), jnp.float32).at[places].add(weighted)

    return lax.map(spread_field, atm_flux).reshape(atm_flux.shape[0], NY, NX)


def reference(atm_flux, margin_source, margin_cell, margin_weight, margin_tile, land_mask, sea_depth, sea_height, transport, tracers):
    ocean_mask = land_mask.astype(jnp.float32)
    forcing = remap_fluxes(atm_flux, margin_source, margin_cell, margin_weight, margin_tile)
    pressure_term = 0.5 * forcing[2]
    wind_x = 0.5 * forcing[0]
    wind_y = 0.5 * forcing[1]
    source = 0.1 * (forcing[6] - forcing[5])
    height, along_flow, across = barotropic(sea_height, transport[0], transport[1], ocean_mask, sea_depth,
                                            pressure_term, wind_x, wind_y, source, SUB)
    moved = horizontal(zero_sides(tracers), zero_sides(ocean_mask), tracers, transport, sea_depth)
    solved = surface_and_mixing(moved, forcing)
    new_tracers = ocean_mask * solved + (1.0 - ocean_mask) * tracers
    return height, jnp.stack([along_flow, across]), new_tracers
```

```python
import functools

import jax
import jax.numpy as jnp
import numpy as np
from jax import lax
from jax.experimental import pallas as pl
from jax.experimental.pallas import tpu as pltpu
from jax.sharding import PartitionSpec as P

SUB = 3
RIM = 8
LANES = 128
AXES = ("comp", "ty", "tx")

damping = 0.95
advect = 0.15
diffuse = 0.1

f32 = jnp.float32
VMEM_LIMIT = 56 * 1024 * 1024


def vmem():
    return pl.BlockSpec(memory_space=pltpu.VMEM)


def smem():
    return pl.BlockSpec(memory_space=pltpu.SMEM)


def pack_kernel(cap, tile_ref, flux_ref, src_ref, cell_ref, weight_ref, out_ref, count_ref):
    tiles = out_ref.shape[0]
    blocks = src_ref.shape[0]
    fields = flux_ref.shape[0]
    width = src_ref.shape[1]

    def clear(t, carry):
        out_ref[t] = jnp.zeros(out_ref.shape[1:], f32)
        count_ref[t] = 0
        return carry

    lax.fori_loop(0, tiles, clear, 0)

    def group(g, carry):
        base = pl.multiple_of(g * 8, 8)
        sources = src_ref[pl.ds(base, 8), :]
        cells = cell_ref[pl.ds(base, 8), :].astype(f32)
        weights = weight_ref[pl.ds(base, 8), :]
        for w in range(4):
            start = pl.multiple_of((g * 4 + w) * width, width)
            window = flux_ref[:, pl.ds(start, width)]
            for half in range(2):
                j = 2 * w + half
                index = jnp.broadcast_to(sources[j : j + 1], (fields, width))
                picked = jnp.take_along_axis(window, index, axis=1)
                t = tile_ref[base + j]
                r = count_ref[t]
                count_ref[t] = r + 1
                at = pl.multiple_of(r * fields, fields)
                out_ref[t, pl.ds(at, fields), :] = picked * weights[j : j + 1]
                out_ref[t, pl.ds(cap * fields + r, 1), :] = cells[j : j + 1]
        return carry

    lax.fori_loop(0, blocks // 8, group, 0)


def pack(margin_tile, atm_flux, margin_source, margin_cell, margin_weight, tiles, cap):
    fields = atm_flux.shape[0]
    rows = cap * fields + -(-cap // 8) * 8
    return pl.pallas_call(
        functools.partial(pack_kernel, cap),
        out_shape=jax.ShapeDtypeStruct((tiles, rows, margin_source.shape[1]), f32),
        in_specs=[smem(), vmem(), vmem(), vmem(), vmem()],
        out_specs=vmem(),
        scratch_shapes=[pltpu.SMEM((tiles,), jnp.int32)],
        compiler_params=pltpu.CompilerParams(vmem_limit_bytes=VMEM_LIMIT),
        cost_estimate=pl.CostEstimate(flops=10_000_000, bytes_accessed=4_000_000, transcendentals=0),
        name="pack",
    )(margin_tile, atm_flux, margin_source, margin_cell, margin_weight)


def scatter_kernel(cap, fields, row_ref, in_ref, forcing_ref, baro_ref, acc_ref):
    owners = in_ref.shape[0]
    width = in_ref.shape[2]
    tile_rows, tile_cols = forcing_ref.shape[1:]
    highs = tile_cols // LANES
    lines = highs * fields
    group = 4 if cap % 4 == 0 else 1

    def clear(y, carry):
        acc_ref[pl.ds(pl.multiple_of(y * lines, lines), lines), :] = jnp.zeros((lines, LANES), f32)
        return carry

    lax.fori_loop(0, tile_rows, clear, 0)
    low_iota = lax.broadcasted_iota(jnp.int32, (LANES, width), 0)

    def owner_step(o, carry):
        cells = in_ref[o, cap * fields : in_ref.shape[1], :].astype(jnp.int32)
        for g in range(cap // group):
            sums = []
            for r in range(g * group, (g + 1) * group):
                row = row_ref[o * cap + r]
                cols = cells[r : r + 1] - row * tile_cols
                high = jnp.broadcast_to(cols // LANES, (fields, width))
                low = jnp.broadcast_to(cols % LANES, (LANES, width))
                onehot = jnp.where(low_iota == low, 1.0, 0.0).astype(jnp.bfloat16)
                values = in_ref[o, r * fields : (r + 1) * fields, :]
                coarse = values.astype(jnp.bfloat16).astype(f32)
                fine = values - coarse
                picks = [high == h for h in range(highs)]
                left = jnp.concatenate(
                    [jnp.where(p, coarse, 0.0) for p in picks]
                    + [jnp.where(p, fine, 0.0) for p in picks],
                    axis=0,
                ).astype(jnp.bfloat16)
                both = lax.dot_general(
                    left, onehot, (((1,), (1,)), ((), ())), preferred_element_type=f32
                )
                sums.append((row, both[:lines] + both[lines:]))
            for row, part in sums:
                at = pl.ds(pl.multiple_of(row * lines, lines), lines)
                acc_ref[at, :] = acc_ref[at, :] + part
        return carry

    lax.fori_loop(0, owners, owner_step, 0)

    def unfold(yb, carry):
        ys = pl.ds(pl.multiple_of(yb * 8, 8), 8)
        for h in range(highs):
            cs = slice(h * LANES, (h + 1) * LANES)
            planes = []
            for f in range(fields):
                part = acc_ref[pl.ds(yb * 8 * lines + h * fields + f, 8, stride=lines), :]
                forcing_ref[f, ys, cs] = part
                planes.append(part)
            baro_ref[0, ys, cs] = 0.5 * planes[2]
            baro_ref[1, ys, cs] = 0.5 * planes[0]
            baro_ref[2, ys, cs] = 0.5 * planes[1]
            baro_ref[3, ys, cs] = 0.1 * (planes[6] - planes[5])
        return carry

    lax.fori_loop(0, tile_rows // 8, unfold, 0)


def scatter(rows, arrived, cap, fields, tile_rows, tile_cols):
    lines = tile_cols // LANES * fields
    return pl.pallas_call(
        functools.partial(scatter_kernel, cap, fields),
        out_shape=(
            jax.ShapeDtypeStruct((fields, tile_rows, tile_cols), f32),
            jax.ShapeDtypeStruct((4, tile_rows, tile_cols), f32),
        ),
        in_specs=[smem(), vmem()],
        out_specs=(vmem(), vmem()),
        scratch_shapes=[pltpu.VMEM((tile_rows * lines, LANES), f32)],
        compiler_params=pltpu.CompilerParams(vmem_limit_bytes=VMEM_LIMIT),
        cost_estimate=pl.CostEstimate(
            flops=2_000_000_000, bytes_accessed=5_000_000, transcendentals=0
        ),
        name="scatter",
    )(rows, arrived)


def edges_kernel(west_ref, east_ref, mask_west_ref, mask_east_ref, first_ref, last_ref):
    planes, rows = west_ref.shape[:2]
    lane = lax.broadcasted_iota(jnp.int32, (rows, LANES), 1)
    for src, mask, dst, col in (
        (west_ref, mask_west_ref, first_ref, 0),
        (east_ref, mask_east_ref, last_ref, LANES - 1),
    ):
        total = jnp.zeros((rows, LANES), f32)
        for p in range(planes):
            total = jnp.where(
                lane == p, jnp.broadcast_to(src[p, :, col : col + 1], (rows, LANES)), total
            )
        edge = mask[:, col : col + 1].astype(f32)
        dst[...] = jnp.where(lane == planes, jnp.broadcast_to(edge, (rows, LANES)), total)


def edge_columns(tracers, land_mask):
    planes, rows, cols = tracers.shape
    end = cols // LANES - 1
    strip = jax.ShapeDtypeStruct((rows, LANES), f32)
    whole = pl.BlockSpec((rows, LANES), lambda i: (0, 0))
    return pl.pallas_call(
        edges_kernel,
        out_shape=(strip, strip),
        grid=(1,),
        in_specs=[
            pl.BlockSpec((planes, rows, LANES), lambda i: (0, 0, 0)),
            pl.BlockSpec((planes, rows, LANES), lambda i: (0, 0, end)),
            pl.BlockSpec((rows, LANES), lambda i: (0, 0)),
            pl.BlockSpec((rows, LANES), lambda i: (0, end)),
        ],
        out_specs=(whole, whole),
        compiler_params=pltpu.CompilerParams(vmem_limit_bytes=VMEM_LIMIT),
        name="edges",
    )(tracers, tracers, land_mask, land_mask)


def tracer_kernel(
    levels,
    tracer_hbm,
    south_ref,
    north_ref,
    west_ref,
    east_ref,
    mask_south_ref,
    mask_north_ref,
    mask_ref,
    depth_ref,
    flow_ref,
    forcing_ref,
    out_ref,
    held,
    mask_held,
    ratio_ref,
    sems,
):
    planes = held.shape[0]
    rows, cols = mask_ref.shape
    steps = rows // 8
    i = pl.program_id(0)

    def chunk(step):
        at = pl.multiple_of(step * 8, 8)
        return pltpu.make_async_copy(
            tracer_hbm.at[:, pl.ds(at, 8), :], held.at[:, pl.ds(at + 8, 8), :], sems.at[step]
        )

    @pl.when(i == 0)
    def _():
        for s in range(steps):
            chunk(s).start()
        for p in range(planes):
            held[p, 7:8, :] = south_ref[p : p + 1, :]
            held[p, rows + 8 : rows + 9, :] = north_ref[p : p + 1, :]
        mask_held[0:8, :] = mask_south_ref[...]
        mask_held[8 : rows + 8, :] = mask_ref[...].astype(f32)
        mask_held[rows + 8 : rows + 16, :] = mask_north_ref[...]
        chunk(0).wait()

    @pl.when(i < steps - 1)
    def _():
        chunk(i + 1).wait()

    base = pl.multiple_of(i * 8, 8)
    here = pl.ds(base + 8, 8)
    lane = lax.broadcasted_iota(jnp.int32, (8, cols), 1) % LANES
    sub = lax.broadcasted_iota(jnp.int32, (8, cols), 0)
    at_first, at_last = lane == 0, lane == LANES - 1
    at_bottom, at_top = sub == 0, sub == 7
    west_edges = west_ref[pl.ds(base, 8), :]
    east_edges = east_ref[pl.ds(base, 8), :]
    pieces = cols // LANES

    def sides(q, below, above, p):
        parts = [q[:, c * LANES : (c + 1) * LANES] for c in range(pieces)]
        up = [pltpu.roll(a, 1, 1) for a in parts]
        down = [pltpu.roll(a, LANES - 1, 1) for a in parts]
        west_edge = jnp.broadcast_to(west_edges[:, p : p + 1], (8, LANES))
        east_edge = jnp.broadcast_to(east_edges[:, p : p + 1], (8, LANES))
        west = jnp.where(
            at_first, jnp.concatenate([west_edge] + up[:-1], 1), jnp.concatenate(up, 1)
        )
        east = jnp.where(
            at_last, jnp.concatenate(down[1:] + [east_edge], 1), jnp.concatenate(down, 1)
        )
        south = jnp.where(at_bottom, jnp.broadcast_to(below, q.shape), pltpu.roll(q, 1, 0))
        north = jnp.where(at_top, jnp.broadcast_to(above, q.shape), pltpu.roll(q, 7, 0))
        return east, west, north, south

    mask = mask_held[here, :]
    mask_e, mask_w, mask_n, mask_s = sides(
        mask, mask_held[pl.ds(base + 7, 1), :], mask_held[pl.ds(base + 16, 1), :], planes
    )
    inverse = 1.0 / depth_ref[...]
    u = flow_ref[0] * inverse
    v = flow_ref[1] * inverse
    ce = mask_e * (diffuse - advect * jnp.minimum(u, 0.0))
    cw = mask_w * (diffuse + advect * jnp.maximum(u, 0.0))
    cn = mask_n * (diffuse - advect * jnp.minimum(v, 0.0))
    cs = mask_s * (diffuse + advect * jnp.maximum(v, 0.0))
    c0 = 1.0 - (ce + cw + cn + cs)

    depths = np.arange(levels, dtype=np.float32)
    absorb = np.exp(-depths / np.float32(3)) - np.exp(-(depths + 1) / np.float32(3))
    fade = np.exp(-depths / np.float32(2))
    stir = 0.5 * forcing_ref[7] * forcing_ref[7]
    sun = 0.5 * forcing_ref[4]
    ratio = None
    last = [None, None]
    lower = None
    for k in range(levels):
        upper = 0.2 + stir * float(fade[k]) if k < levels - 1 else None
        pivot = 1.0
        if upper is not None:
            pivot = pivot + upper
        if lower is not None:
            pivot = pivot + lower + lower * ratio
        scale = 1.0 / pivot
        if upper is not None:
            ratio = -upper * scale
            ratio_ref[k] = ratio
        for t in range(2):
            p = t * levels + k
            q = held[p, here, :]
            qe, qw, qn, qs = sides(
                q, held[p, pl.ds(base + 7, 1), :], held[p, pl.ds(base + 16, 1), :], p
            )
            side = c0 * q + ce * qe + cw * qw + cn * qn + cs * qs
            if t == 0:
                side = side + sun * float(absorb[k])
                if k == 0:
                    side = side + 0.5 * forcing_ref[3]
            elif k == 0:
                side = side + (0.5 * forcing_ref[5] - 0.3 * forcing_ref[6])
            if lower is not None:
                side = side + lower * last[t]
            last[t] = side * scale
            out_ref[p] = last[t]
        lower = upper
    ocean = mask > 0.5
    for k in range(levels - 1, -1, -1):
        for t in range(2):
            p = t * levels + k
            if k < levels - 1:
                last[t] = out_ref[p] - ratio_ref[k] * last[t]
            out_ref[p] = jnp.where(ocean, last[t], held[p, here, :])


def tracer_step(
    levels, tracers, south, north, west, east, mask_south, mask_north, mask, depth, flow, forcing
):
    planes, rows, cols = tracers.shape

    def band(*lead):
        zeros = (0,) * len(lead)
        return pl.BlockSpec((*lead, 8, cols), lambda i: (*zeros, i, 0))

    def full(a):
        zeros = (0,) * a.ndim
        return pl.BlockSpec(a.shape, lambda i: zeros)

    return pl.pallas_call(
        functools.partial(tracer_kernel, levels),
        out_shape=jax.ShapeDtypeStruct(tracers.shape, f32),
        grid=(rows // 8,),
        in_specs=[
            pl.BlockSpec(memory_space=pl.ANY),
            full(south),
            full(north),
            full(west),
            full(east),
            full(mask_south),
            full(mask_north),
            full(mask),
            band(),
            band(2),
            band(forcing.shape[0]),
        ],
        out_specs=band(planes),
        scratch_shapes=[
            pltpu.VMEM((planes, rows + 16, cols), f32),
            pltpu.VMEM((rows + 16, cols), f32),
            pltpu.VMEM((levels, 8, cols), f32),
            pltpu.SemaphoreType.DMA((rows // 8,)),
        ],
        compiler_params=pltpu.CompilerParams(
            vmem_limit_bytes=VMEM_LIMIT, dimension_semantics=("arbitrary",)
        ),
        cost_estimate=pl.CostEstimate(
            flops=100_000_000, bytes_accessed=40_000_000, transcendentals=0
        ),
        name="tracer",
    )(tracers, south, north, west, east, mask_south, mask_north, mask, depth, flow, forcing)


def baro_kernel(
    height_ref,
    flow_ref,
    mask_ref,
    depth_ref,
    baro_ref,
    south_ref,
    north_ref,
    west_ref,
    east_ref,
    fs_ref,
    fn_ref,
    fw_ref,
    fe_ref,
    fsw_ref,
    fse_ref,
    fnw_ref,
    fne_ref,
    height_out,
    flow_out,
):
    rows, cols = height_ref.shape

    def still(k, tile):
        middle = jnp.concatenate([south_ref[k], tile, north_ref[k]], 0)
        return jnp.concatenate([west_ref[k], middle, east_ref[k]], 1)

    def forced(k):
        low = jnp.concatenate([fsw_ref[k], fs_ref[k], fse_ref[k]], 1)
        mid = jnp.concatenate([fw_ref[k], baro_ref[k], fe_ref[k]], 1)
        top = jnp.concatenate([fnw_ref[k], fn_ref[k], fne_ref[k]], 1)
        return jnp.concatenate([low, mid, top], 0)

    height = still(0, height_ref[...])
    along = still(1, flow_ref[0])
    across = still(2, flow_ref[1])
    mask = still(3, mask_ref[...].astype(f32))
    bottom = -0.5 * still(4, depth_ref[...])
    pressure, wind_x, wind_y, source = [forced(k) for k in range(4)]
    tall, wide = height.shape

    def slope_x(a):
        return pltpu.roll(a, wide - 1, 1) - pltpu.roll(a, 1, 1)

    def slope_y(a):
        return pltpu.roll(a, tall - 1, 0) - pltpu.roll(a, 1, 0)

    for _ in range(SUB):
        level = mask * (height + pressure)
        along = mask * (damping * along + (bottom * slope_x(level) + wind_x))
        across = mask * (damping * across + (bottom * slope_y(level) + wind_y))
        height = mask * (height - 0.5 * (slope_x(along) + slope_y(across)) + source)
    inner = (slice(RIM, RIM + rows), slice(LANES, LANES + cols))
    height_out[...] = height[inner]
    flow_out[0] = along[inner]
    flow_out[1] = across[inner]


def local(
    ny,
    nx,
    atm_flux,
    margin_source,
    margin_cell,
    margin_weight,
    margin_tile,
    land_mask,
    sea_depth,
    sea_height,
    transport,
    tracers,
):
    levels = tracers.shape[1]
    tile_rows, tile_cols = sea_height.shape
    fields = atm_flux.shape[0]
    tiles = ny * nx
    cap = 2 * margin_source.shape[0] // tiles

    def from_side(a, dy, dx):
        perm = [
            ((y + dy) * nx + x + dx, y * nx + x)
            for y in range(ny)
            for x in range(nx)
            if 0 <= y + dy < ny and 0 <= x + dx < nx
        ]
        return lax.ppermute(a, AXES, perm)

    flat = tracers.reshape(2 * levels, tile_rows, tile_cols)
    still = jnp.stack(
        [sea_height, transport[0], transport[1], land_mask.astype(f32), sea_depth]
    )
    count = still.shape[0]

    def lines(edge, band):
        return jnp.concatenate([edge, band.reshape(count * RIM, tile_cols)], 0)

    planes = 2 * levels
    got_s = from_side(lines(flat[:, -1], still[:, -RIM:]), -1, 0)
    got_n = from_side(lines(flat[:, 0], still[:, :RIM]), 1, 0)
    still_s = got_s[planes:].reshape(count, RIM, tile_cols)
    still_n = got_n[planes:].reshape(count, RIM, tile_cols)
    tall = jnp.concatenate([still_s, still, still_n], 1)
    first, last = edge_columns(flat, land_mask)
    ext = (tile_rows + 2 * RIM) * count

    def columns(edge, band):
        return jnp.concatenate([edge, band.reshape(ext, LANES)], 0)

    got_w = from_side(columns(last, tall[:, :, -LANES:]), 0, -1)
    got_e = from_side(columns(first, tall[:, :, :LANES]), 0, 1)
    still_w = got_w[tile_rows:].reshape(count, -1, LANES)
    still_e = got_e[tile_rows:].reshape(count, -1, LANES)

    outgoing = pack(
        margin_tile[:, 0], atm_flux, margin_source, margin_cell, margin_weight, tiles, cap
    )
    arrived = lax.all_to_all(outgoing, AXES, split_axis=0, concat_axis=0, tiled=True)
    slot_rows = arrived[:, cap * fields : cap * fields + cap, 0].astype(jnp.int32) // tile_cols
    forcing, baro = scatter(
        slot_rows.reshape(-1), arrived, cap, fields, tile_rows, tile_cols
    )

    low, high = slice(None, RIM), slice(-RIM, None)
    left, right = slice(None, LANES), slice(-LANES, None)
    halo = [
        from_side(baro[:, high], -1, 0),
        from_side(baro[:, low], 1, 0),
        from_side(baro[:, :, right], 0, -1),
        from_side(baro[:, :, left], 0, 1),
        from_side(baro[:, high, right], -1, -1),
        from_side(baro[:, high, left], -1, 1),
        from_side(baro[:, low, right], 1, -1),
        from_side(baro[:, low, left], 1, 1),
    ]
    new_tracers = tracer_step(
        levels,
        flat,
        got_s[:planes],
        got_n[:planes],
        got_w[:tile_rows],
        got_e[:tile_rows],
        still_s[3],
        still_n[3],
        land_mask,
        sea_depth,
        transport,
        forcing,
    )
    height, flow = pl.pallas_call(
        baro_kernel,
        out_shape=(
            jax.ShapeDtypeStruct(sea_height.shape, f32),
            jax.ShapeDtypeStruct(transport.shape, f32),
        ),
        in_specs=[vmem()] * 17,
        out_specs=(vmem(), vmem()),
        compiler_params=pltpu.CompilerParams(vmem_limit_bytes=VMEM_LIMIT),
        name="baro",
    )(
        sea_height,
        transport,
        land_mask,
        sea_depth,
        baro,
        still_s,
        still_n,
        still_w,
        still_e,
        *halo,
    )
    return (height, flow, new_tracers.reshape(tracers.shape))


def solution(mesh):
    in_specs = (
        P(None, AXES),
        P(AXES, None),
        P(AXES, None),
        P(AXES, None),
        P(AXES, None),
        P(("comp", "ty"), "tx"),
        P(("comp", "ty"), "tx"),
        P(("comp", "ty"), "tx"),
        P(None, ("comp", "ty"), "tx"),
        P(None, None, ("comp", "ty"), "tx"),
    )
    out_specs = (
        P(("comp", "ty"), "tx"),
        P(None, ("comp", "ty"), "tx"),
        P(None, None, ("comp", "ty"), "tx"),
    )
    ny = mesh.shape["comp"] * mesh.shape["ty"]
    nx = mesh.shape["tx"]
    body = functools.partial(local, ny, nx)
    return jax.shard_map(body, mesh=mesh, in_specs=in_specs, out_specs=out_specs, check_vma=False)
```

```python
import functools

import jax
import jax.numpy as jnp
import numpy as np
from jax import lax
from jax.experimental import pallas as pl
from jax.experimental.pallas import tpu as pltpu
from jax.sharding import PartitionSpec as P

SUB = 3
RIM = 8
LANES = 128
AXES = ("comp", "ty", "tx")

damping = 0.95
advect = 0.15
diffuse = 0.1

f32 = jnp.float32
VMEM_LIMIT = 56 * 1024 * 1024


def vmem():
    return pl.BlockSpec(memory_space=pltpu.VMEM)


def smem():
    return pl.BlockSpec(memory_space=pltpu.SMEM)


def pack_kernel(cap, tile_ref, flux_ref, src_ref, cell_ref, weight_ref, *rest):
    *parts, out_ref, count_ref = rest
    tiles = parts[0].shape[0]
    share = cap // len(parts)
    blocks = src_ref.shape[0]
    fields = flux_ref.shape[0]
    width = src_ref.shape[1]

    def clear(t, carry):
        for c in range(len(parts)):
            out_ref[c * tiles + t] = jnp.zeros(out_ref.shape[1:], f32)
        count_ref[t] = 0
        return carry

    lax.fori_loop(0, tiles, clear, 0)

    def group(g, carry):
        base = pl.multiple_of(g * 8, 8)
        sources = src_ref[pl.ds(base, 8), :]
        cells = cell_ref[pl.ds(base, 8), :].astype(f32)
        weights = weight_ref[pl.ds(base, 8), :]
        for w in range(4):
            start = pl.multiple_of((g * 4 + w) * width, width)
            window = flux_ref[:, pl.ds(start, width)]
            for half in range(2):
                j = 2 * w + half
                index = jnp.broadcast_to(sources[j : j + 1], (fields, width))
                picked = jnp.take_along_axis(window, index, axis=1)
                t = tile_ref[base + j]
                r = count_ref[t]
                count_ref[t] = r + 1
                slot = r % share
                lead = (r // share) * tiles + t
                at = pl.multiple_of(slot * fields, fields)
                out_ref[lead, pl.ds(at, fields), :] = picked * weights[j : j + 1]
                out_ref[lead, pl.ds(share * fields + slot, 1), :] = cells[j : j + 1]
        return carry

    lax.fori_loop(0, blocks // 8, group, 0)
    for c, part in enumerate(parts):

        def move(t, carry, c=c, part=part):
            part[t] = out_ref[c * tiles + t]
            return carry

        lax.fori_loop(0, tiles, move, 0)


def pack(margin_tile, atm_flux, margin_source, margin_cell, margin_weight, tiles, cap, parts):
    fields = atm_flux.shape[0]
    share = cap // parts
    rows = share * fields + -(-share // 8) * 8
    width = margin_source.shape[1]
    return pl.pallas_call(
        functools.partial(pack_kernel, cap),
        out_shape=[jax.ShapeDtypeStruct((tiles, rows, width), f32)] * parts,
        in_specs=[smem(), vmem(), vmem(), vmem(), vmem()],
        out_specs=[vmem()] * parts,
        scratch_shapes=[
            pltpu.VMEM((parts * tiles, rows, width), f32),
            pltpu.SMEM((tiles,), jnp.int32),
        ],
        compiler_params=pltpu.CompilerParams(vmem_limit_bytes=VMEM_LIMIT),
        cost_estimate=pl.CostEstimate(flops=10_000_000, bytes_accessed=4_000_000, transcendentals=0),
        name="pack",
    )(margin_tile, atm_flux, margin_source, margin_cell, margin_weight)


def scatter_kernel(cap, fields, tile_rows, tile_cols, start, finish, row_ref, in_ref, *rest):
    if finish:
        forcing_ref, baro_ref, acc_ref = rest[-3:]
    else:
        acc_ref = rest[-1]
    owners = in_ref.shape[0]
    width = in_ref.shape[2]
    highs = tile_cols // LANES
    lines = highs * fields
    group = 4 if cap % 4 == 0 else 1

    def clear(y, carry):
        at = pl.ds(pl.multiple_of(y * lines, lines), lines)
        acc_ref[at, :] = jnp.zeros((lines, LANES), f32) if start else rest[0][at, :]
        return carry

    lax.fori_loop(0, tile_rows, clear, 0)
    low_iota = lax.broadcasted_iota(jnp.int32, (LANES, width), 0)

    def owner_step(o, carry):
        cells = in_ref[o, cap * fields : in_ref.shape[1], :].astype(jnp.int32)
        for g in range(cap // group):
            sums = []
            for r in range(g * group, (g + 1) * group):
                row = row_ref[o * cap + r]
                cols = cells[r : r + 1] - row * tile_cols
                high = jnp.broadcast_to(cols // LANES, (fields, width))
                low = jnp.broadcast_to(cols % LANES, (LANES, width))
                onehot = jnp.where(low_iota == low, 1.0, 0.0).astype(jnp.bfloat16)
                values = in_ref[o, r * fields : (r + 1) * fields, :]
                coarse = values.astype(jnp.bfloat16).astype(f32)
                fine = values - coarse
                picks = [high == h for h in range(highs)]
                left = jnp.concatenate(
                    [jnp.where(p, coarse, 0.0) for p in picks]
                    + [jnp.where(p, fine, 0.0) for p in picks],
                    axis=0,
                ).astype(jnp.bfloat16)
                both = lax.dot_general(
                    left, onehot, (((1,), (1,)), ((), ())), preferred_element_type=f32
                )
                sums.append((row, both[:lines] + both[lines:]))
            for row, part in sums:
                at = pl.ds(pl.multiple_of(row * lines, lines), lines)
                acc_ref[at, :] = acc_ref[at, :] + part
        return carry

    lax.fori_loop(0, owners, owner_step, 0)

    if not finish:
        return

    def unfold(yb, carry):
        ys = pl.ds(pl.multiple_of(yb * 8, 8), 8)
        for h in range(highs):
            cs = slice(h * LANES, (h + 1) * LANES)
            planes = []
            for f in range(fields):
                part = acc_ref[pl.ds(yb * 8 * lines + h * fields + f, 8, stride=lines), :]
                forcing_ref[f, ys, cs] = part
                planes.append(part)
            baro_ref[0, ys, cs] = 0.5 * planes[2]
            baro_ref[1, ys, cs] = 0.5 * planes[0]
            baro_ref[2, ys, cs] = 0.5 * planes[1]
            baro_ref[3, ys, cs] = 0.1 * (planes[6] - planes[5])
        return carry

    lax.fori_loop(0, tile_rows // 8, unfold, 0)


def scatter(rows, arrived, total, cap, fields, tile_rows, tile_cols, finish):
    lines = tile_cols // LANES * fields
    sums = (tile_rows * lines, LANES)
    extra = [] if total is None else [total]
    if finish:
        out_shape = [
            jax.ShapeDtypeStruct((fields, tile_rows, tile_cols), f32),
            jax.ShapeDtypeStruct((4, tile_rows, tile_cols), f32),
        ]
    else:
        out_shape = [jax.ShapeDtypeStruct(sums, f32)]
    return pl.pallas_call(
        functools.partial(
            scatter_kernel, cap, fields, tile_rows, tile_cols, total is None, finish
        ),
        out_shape=out_shape,
        in_specs=[smem(), vmem()] + [vmem()] * len(extra),
        out_specs=[vmem()] * len(out_shape),
        scratch_shapes=[pltpu.VMEM(sums, f32)] if finish else [],
        compiler_params=pltpu.CompilerParams(vmem_limit_bytes=VMEM_LIMIT),
        cost_estimate=pl.CostEstimate(
            flops=2_000_000_000, bytes_accessed=20_000_000, transcendentals=0
        ),
        name="scatter",
    )(rows, arrived, *extra)


def edges_kernel(
    west_ref, east_ref, low_ref, high_ref, mask_west_ref, mask_east_ref,
    first_ref, last_ref, bottom_ref, top_ref,
):
    planes, rows = west_ref.shape[:2]
    lane = lax.broadcasted_iota(jnp.int32, (rows, LANES), 1)
    for src, mask, dst, col in (
        (west_ref, mask_west_ref, first_ref, 0),
        (east_ref, mask_east_ref, last_ref, LANES - 1),
    ):
        total = jnp.zeros((rows, LANES), f32)
        for p in range(planes):
            total = jnp.where(
                lane == p, jnp.broadcast_to(src[p, :, col : col + 1], (rows, LANES)), total
            )
        edge = mask[:, col : col + 1].astype(f32)
        dst[...] = jnp.where(lane == planes, jnp.broadcast_to(edge, (rows, LANES)), total)
    for p in range(planes):
        bottom_ref[p : p + 1, :] = low_ref[p, 0:1, :]
        top_ref[p : p + 1, :] = high_ref[p, 7:8, :]


def tracer_edges(tracers, land_mask):
    planes, rows, cols = tracers.shape
    end = cols // LANES - 1
    top = rows // 8 - 1
    strip = jax.ShapeDtypeStruct((rows, LANES), f32)
    line = jax.ShapeDtypeStruct((planes, cols), f32)
    whole = pl.BlockSpec((rows, LANES), lambda i: (0, 0))
    wide = pl.BlockSpec((planes, cols), lambda i: (0, 0))
    return pl.pallas_call(
        edges_kernel,
        out_shape=(strip, strip, line, line),
        grid=(1,),
        in_specs=[
            pl.BlockSpec((planes, rows, LANES), lambda i: (0, 0, 0)),
            pl.BlockSpec((planes, rows, LANES), lambda i: (0, 0, end)),
            pl.BlockSpec((planes, 8, cols), lambda i: (0, 0, 0)),
            pl.BlockSpec((planes, 8, cols), lambda i: (0, top, 0)),
            pl.BlockSpec((rows, LANES), lambda i: (0, 0)),
            pl.BlockSpec((rows, LANES), lambda i: (0, end)),
        ],
        out_specs=(whole, whole, wide, wide),
        compiler_params=pltpu.CompilerParams(vmem_limit_bytes=VMEM_LIMIT),
        cost_estimate=pl.CostEstimate(flops=1_000_000, bytes_accessed=5_000_000, transcendentals=0),
        name="edges",
    )(tracers, tracers, tracers, tracers, land_mask, land_mask)


WAYS = ((1, 0), (-1, 0), (0, 1), (0, -1), (1, 1), (1, -1), (-1, 1), (-1, -1))


def exchange_kernel(mesh_shape, extras, *refs):
    comps, depth, nx = mesh_shape
    ny = comps * depth
    band, lines = refs[0], refs[1 : 1 + extras]
    outs = refs[1 + extras : 1 + 2 * extras + len(WAYS)]
    send_sems, recv_sems = refs[-2:]
    rows, cols = band.shape[1:]
    y = lax.axis_index("comp") * depth + lax.axis_index("ty")
    x = lax.axis_index("tx")

    def inside(dy, dx):
        return (y + dy >= 0) & (y + dy < ny) & (x + dx >= 0) & (x + dx < nx)

    def place(dy, dx):
        return ((y + dy) // depth, (y + dy) % depth, x + dx)

    barrier = pltpu.get_barrier_semaphore()
    near = jnp.int32(0)
    for way in WAYS:
        near = near + inside(*way).astype(jnp.int32)

        @pl.when(inside(*way))
        def _(way=way):
            pl.semaphore_signal(
                barrier, inc=1, device_id=place(*way), device_id_type=pl.DeviceIdType.MESH
            )

    pl.semaphore_wait(barrier, near)

    def pieces():
        for k, (dy, dx) in enumerate(WAYS):
            start_y = rows - RIM if dy == 1 else 0
            start_x = cols - LANES if dx == 1 else 0
            tall = RIM if dy else rows
            wide = LANES if dx else cols
            yield (dy, dx), band.at[:, pl.ds(start_y, tall), pl.ds(start_x, wide)]
        for k in range(extras):
            yield WAYS[k], lines[k]

    copies = []
    for k, (way, src) in enumerate(pieces()):
        dst = outs[k]

        def copy(way=way, src=src, dst=dst, k=k):
            return pltpu.make_async_remote_copy(
                src_ref=src,
                dst_ref=dst,
                send_sem=send_sems.at[k],
                recv_sem=recv_sems.at[k],
                device_id=place(*way),
                device_id_type=pl.DeviceIdType.MESH,
            )

        sends, gets = inside(*way), inside(-way[0], -way[1])

        @pl.when(sends)
        def _(copy=copy):
            copy().start()

        @pl.when(jnp.logical_not(gets))
        def _(dst=dst):
            dst[...] = jnp.zeros(dst.shape, f32)

        copies.append((copy, sends, gets))
    for copy, sends, gets in copies:

        @pl.when(sends)
        def _(copy=copy):
            copy().wait_send()

        @pl.when(gets)
        def _(copy=copy):
            copy().wait_recv()


def exchange(mesh_shape, band, lines, number):
    count, rows, cols = band.shape
    shapes = [
        (count, RIM if dy else rows, LANES if dx else cols) for dy, dx in WAYS
    ] + [a.shape for a in lines]
    return pl.pallas_call(
        functools.partial(exchange_kernel, mesh_shape, len(lines)),
        out_shape=[jax.ShapeDtypeStruct(s, f32) for s in shapes],
        in_specs=[vmem()] * (1 + len(lines)),
        out_specs=[vmem()] * len(shapes),
        scratch_shapes=[
            pltpu.SemaphoreType.DMA((len(shapes),)),
            pltpu.SemaphoreType.DMA((len(shapes),)),
        ],
        compiler_params=pltpu.CompilerParams(
            collective_id=number, has_side_effects=True, vmem_limit_bytes=VMEM_LIMIT
        ),
        cost_estimate=pl.CostEstimate(flops=1000, bytes_accessed=5_000_000, transcendentals=0),
        name="exchange",
    )(band, *lines)


def advect_kernel(
    tracer_hbm,
    south_ref,
    north_ref,
    west_ref,
    east_ref,
    mask_south_ref,
    mask_north_ref,
    mask_ref,
    depth_ref,
    flow_ref,
    out_ref,
    held,
    mask_held,
    sems,
):
    planes = held.shape[0]
    rows, cols = mask_ref.shape
    steps = rows // 8
    i = pl.program_id(0)

    def chunk(step):
        at = pl.multiple_of(step * 8, 8)
        return pltpu.make_async_copy(
            tracer_hbm.at[:, pl.ds(at, 8), :], held.at[:, pl.ds(at + 8, 8), :], sems.at[step]
        )

    @pl.when(i == 0)
    def _():
        for s in range(steps):
            chunk(s).start()
        for p in range(planes):
            held[p, 7:8, :] = south_ref[p : p + 1, :]
            held[p, rows + 8 : rows + 9, :] = north_ref[p : p + 1, :]
        mask_held[0:8, :] = mask_south_ref[...]
        mask_held[8 : rows + 8, :] = mask_ref[...].astype(f32)
        mask_held[rows + 8 : rows + 16, :] = mask_north_ref[...]
        chunk(0).wait()

    @pl.when(i < steps - 1)
    def _():
        chunk(i + 1).wait()

    base = pl.multiple_of(i * 8, 8)
    here = pl.ds(base + 8, 8)
    lane = lax.broadcasted_iota(jnp.int32, (8, cols), 1) % LANES
    sub = lax.broadcasted_iota(jnp.int32, (8, cols), 0)
    at_first, at_last = lane == 0, lane == LANES - 1
    at_bottom, at_top = sub == 0, sub == 7
    west_edges = west_ref[pl.ds(base, 8), :]
    east_edges = east_ref[pl.ds(base, 8), :]
    pieces = cols // LANES

    def sides(q, below, above, p):
        parts = [q[:, c * LANES : (c + 1) * LANES] for c in range(pieces)]
        up = [pltpu.roll(a, 1, 1) for a in parts]
        down = [pltpu.roll(a, LANES - 1, 1) for a in parts]
        west_edge = jnp.broadcast_to(west_edges[:, p : p + 1], (8, LANES))
        east_edge = jnp.broadcast_to(east_edges[:, p : p + 1], (8, LANES))
        west = jnp.where(
            at_first, jnp.concatenate([west_edge] + up[:-1], 1), jnp.concatenate(up, 1)
        )
        east = jnp.where(
            at_last, jnp.concatenate(down[1:] + [east_edge], 1), jnp.concatenate(down, 1)
        )
        south = jnp.where(at_bottom, jnp.broadcast_to(below, q.shape), pltpu.roll(q, 1, 0))
        north = jnp.where(at_top, jnp.broadcast_to(above, q.shape), pltpu.roll(q, 7, 0))
        return east, west, north, south

    mask = mask_held[here, :]
    mask_e, mask_w, mask_n, mask_s = sides(
        mask, mask_held[pl.ds(base + 7, 1), :], mask_held[pl.ds(base + 16, 1), :], planes
    )
    inverse = 1.0 / depth_ref[...]
    u = flow_ref[0] * inverse
    v = flow_ref[1] * inverse
    ce = mask_e * (diffuse - advect * jnp.minimum(u, 0.0))
    cw = mask_w * (diffuse + advect * jnp.maximum(u, 0.0))
    cn = mask_n * (diffuse - advect * jnp.minimum(v, 0.0))
    cs = mask_s * (diffuse + advect * jnp.maximum(v, 0.0))
    c0 = 1.0 - (ce + cw + cn + cs)

    ocean = mask > 0.5
    for p in range(planes):
        q = held[p, here, :]
        qe, qw, qn, qs = sides(
            q, held[p, pl.ds(base + 7, 1), :], held[p, pl.ds(base + 16, 1), :], p
        )
        moved = c0 * q + ce * qe + cw * qw + cn * qn + cs * qs
        out_ref[p] = jnp.where(ocean, moved, q)


def solve_kernel(levels, moved_ref, mask_ref, forcing_ref, out_ref, ratio_ref):
    depths = np.arange(levels, dtype=np.float32)
    absorb = np.exp(-depths / np.float32(3)) - np.exp(-(depths + 1) / np.float32(3))
    fade = np.exp(-depths / np.float32(2))
    ocean = mask_ref[...].astype(f32)
    floor = 0.2 * ocean
    stir = (0.5 * ocean) * forcing_ref[7] * forcing_ref[7]
    sun = (0.5 * ocean) * forcing_ref[4]
    ratio = None
    last = [None, None]
    lower = None
    for k in range(levels):
        upper = floor + stir * float(fade[k]) if k < levels - 1 else None
        pivot = 1.0
        if upper is not None:
            pivot = pivot + upper
        if lower is not None:
            pivot = pivot + lower + lower * ratio
        scale = 1.0 / pivot
        if upper is not None:
            ratio = -upper * scale
            ratio_ref[k] = ratio
        for t in range(2):
            p = t * levels + k
            side = moved_ref[p]
            if t == 0:
                side = side + sun * float(absorb[k])
                if k == 0:
                    side = side + (0.5 * ocean) * forcing_ref[3]
            elif k == 0:
                side = side + ocean * (0.5 * forcing_ref[5] - 0.3 * forcing_ref[6])
            if lower is not None:
                side = side + lower * last[t]
            last[t] = side * scale
            out_ref[p] = last[t]
        lower = upper
    for k in range(levels - 2, -1, -1):
        for t in range(2):
            p = t * levels + k
            last[t] = out_ref[p] - ratio_ref[k] * last[t]
            out_ref[p] = last[t]


def solve_step(levels, moved, mask, forcing):
    planes, rows, cols = moved.shape

    def band(*lead):
        zeros = (0,) * len(lead)
        return pl.BlockSpec((*lead, 8, cols), lambda i: (*zeros, i, 0))

    return pl.pallas_call(
        functools.partial(solve_kernel, levels),
        out_shape=jax.ShapeDtypeStruct(moved.shape, f32),
        grid=(rows // 8,),
        in_specs=[band(planes), band(), band(forcing.shape[0])],
        out_specs=band(planes),
        scratch_shapes=[pltpu.VMEM((levels, 8, cols), f32)],
        compiler_params=pltpu.CompilerParams(
            vmem_limit_bytes=VMEM_LIMIT, dimension_semantics=("arbitrary",)
        ),
        cost_estimate=pl.CostEstimate(
            flops=30_000_000, bytes_accessed=25_000_000, transcendentals=0
        ),
        name="solve",
    )(moved, mask, forcing)


def advect_step(
    tracers, south, north, west, east, mask_south, mask_north, mask, depth, flow
):
    planes, rows, cols = tracers.shape

    def band(*lead):
        zeros = (0,) * len(lead)
        return pl.BlockSpec((*lead, 8, cols), lambda i: (*zeros, i, 0))

    def full(a):
        zeros = (0,) * a.ndim
        return pl.BlockSpec(a.shape, lambda i: zeros)

    return pl.pallas_call(
        advect_kernel,
        out_shape=jax.ShapeDtypeStruct(tracers.shape, f32),
        grid=(rows // 8,),
        in_specs=[
            pl.BlockSpec(memory_space=pl.ANY),
            full(south),
            full(north),
            full(west),
            full(east),
            full(mask_south),
            full(mask_north),
            full(mask),
            band(),
            band(2),
        ],
        out_specs=band(planes),
        scratch_shapes=[
            pltpu.VMEM((planes, rows + 16, cols), f32),
            pltpu.VMEM((rows + 16, cols), f32),
            pltpu.SemaphoreType.DMA((rows // 8,)),
        ],
        compiler_params=pltpu.CompilerParams(
            vmem_limit_bytes=VMEM_LIMIT, dimension_semantics=("arbitrary",)
        ),
        cost_estimate=pl.CostEstimate(
            flops=100_000_000, bytes_accessed=40_000_000, transcendentals=0
        ),
        name="advect",
    )(tracers, south, north, west, east, mask_south, mask_north, mask, depth, flow)


def baro_kernel(
    height_ref,
    flow_ref,
    mask_ref,
    depth_ref,
    baro_ref,
    *refs,
):
    rows, cols = height_ref.shape
    height_out, flow_out = refs[-2:]

    def widen(k, tile, around):
        s, n, w, e, sw, se, nw, ne = [a[k] for a in around]
        low = jnp.concatenate([sw, s, se], 1)
        mid = jnp.concatenate([w, tile, e], 1)
        top = jnp.concatenate([nw, n, ne], 1)
        return jnp.concatenate([low, mid, top], 0)

    def still(k, tile):
        return widen(k, tile, refs[:8])

    def forced(k):
        return widen(k, baro_ref[k], refs[8:16])

    height = still(0, height_ref[...])
    along = still(1, flow_ref[0])
    across = still(2, flow_ref[1])
    mask = still(3, mask_ref[...].astype(f32))
    bottom = -0.5 * still(4, depth_ref[...])
    pressure, wind_x, wind_y, source = [forced(k) for k in range(4)]
    tall, wide = height.shape

    def slope_x(a):
        return pltpu.roll(a, wide - 1, 1) - pltpu.roll(a, 1, 1)

    def slope_y(a):
        return pltpu.roll(a, tall - 1, 0) - pltpu.roll(a, 1, 0)

    for _ in range(SUB):
        level = mask * (height + pressure)
        along = mask * (damping * along + (bottom * slope_x(level) + wind_x))
        across = mask * (damping * across + (bottom * slope_y(level) + wind_y))
        height = mask * (height - 0.5 * (slope_x(along) + slope_y(across)) + source)
    inner = (slice(RIM, RIM + rows), slice(LANES, LANES + cols))
    height_out[...] = height[inner]
    flow_out[0] = along[inner]
    flow_out[1] = across[inner]


def local(
    mesh_shape,
    atm_flux,
    margin_source,
    margin_cell,
    margin_weight,
    margin_tile,
    land_mask,
    sea_depth,
    sea_height,
    transport,
    tracers,
):
    levels = tracers.shape[1]
    tile_rows, tile_cols = sea_height.shape
    fields = atm_flux.shape[0]
    tiles = mesh_shape[0] * mesh_shape[1] * mesh_shape[2]
    cap = 2 * margin_source.shape[0] // tiles
    parts = 2 if cap % 2 == 0 else 1
    share = cap // parts

    outgoing = pack(
        margin_tile[:, 0], atm_flux, margin_source, margin_cell, margin_weight, tiles, cap, parts
    )
    arrivals = [
        lax.all_to_all(a, AXES, split_axis=0, concat_axis=0, tiled=True) for a in outgoing
    ]

    flat = tracers.reshape(2 * levels, tile_rows, tile_cols)
    still = jnp.stack(
        [sea_height, transport[0], transport[1], land_mask.astype(f32), sea_depth]
    )
    first, last, bottom, top = tracer_edges(flat, land_mask)
    *rim, south, north, west, east = exchange(mesh_shape, still, (top, bottom, last, first), 0)
    moved = advect_step(
        flat, south, north, west, east, rim[0][3], rim[1][3], land_mask, sea_depth, transport
    )

    total = None
    for c, arrived in enumerate(arrivals):
        cells = arrived[:, share * fields : share * fields + share, 0]
        slot_rows = cells.astype(jnp.int32) // tile_cols
        done = scatter(
            slot_rows.reshape(-1),
            arrived,
            total,
            share,
            fields,
            tile_rows,
            tile_cols,
            c == parts - 1,
        )
        total = done[0]
    forcing, baro = done
    halo = exchange(mesh_shape, baro, (), 1)
    new_tracers = solve_step(levels, moved, land_mask, forcing)
    height, flow = pl.pallas_call(
        baro_kernel,
        out_shape=(
            jax.ShapeDtypeStruct(sea_height.shape, f32),
            jax.ShapeDtypeStruct(transport.shape, f32),
        ),
        in_specs=[vmem()] * (5 + 2 * len(WAYS)),
        out_specs=(vmem(), vmem()),
        compiler_params=pltpu.CompilerParams(vmem_limit_bytes=VMEM_LIMIT),
        cost_estimate=pl.CostEstimate(flops=10_000_000, bytes_accessed=8_000_000, transcendentals=0),
        name="baro",
    )(sea_height, transport, land_mask, sea_depth, baro, *rim, *halo)
    return (height, flow, new_tracers.reshape(tracers.shape))


def solution(mesh):
    in_specs = (
        P(None, AXES),
        P(AXES, None),
        P(AXES, None),
        P(AXES, None),
        P(AXES, None),
        P(("comp", "ty"), "tx"),
        P(("comp", "ty"), "tx"),
        P(("comp", "ty"), "tx"),
        P(None, ("comp", "ty"), "tx"),
        P(None, None, ("comp", "ty"), "tx"),
    )
    out_specs = (
        P(("comp", "ty"), "tx"),
        P(None, ("comp", "ty"), "tx"),
        P(None, None, ("comp", "ty"), "tx"),
    )
    body = functools.partial(local, tuple(mesh.shape[axis] for axis in AXES))
    return jax.shard_map(body, mesh=mesh, in_specs=in_specs, out_specs=out_specs, check_vma=False)
```

```python
import functools

import jax
import jax.numpy as jnp
import numpy as np
from jax import lax
from jax.experimental import pallas as pl
from jax.experimental.pallas import tpu as pltpu
from jax.sharding import PartitionSpec as P

SUB = 3
RIM = 8
LANES = 128
AXES = ("comp", "ty", "tx")

damping = 0.95
advect = 0.15
diffuse = 0.1

f32 = jnp.float32
VMEM_LIMIT = 56 * 1024 * 1024


def vmem():
    return pl.BlockSpec(memory_space=pltpu.VMEM)


def smem():
    return pl.BlockSpec(memory_space=pltpu.SMEM)


def pack_kernel(cap, tile_ref, flux_ref, src_ref, cell_ref, weight_ref, *rest):
    *parts, out_ref, count_ref = rest
    tiles = parts[0].shape[0]
    share = cap // len(parts)
    blocks = src_ref.shape[0]
    fields = flux_ref.shape[0]
    width = src_ref.shape[1]

    def clear(t, carry):
        for c in range(len(parts)):
            out_ref[c * tiles + t] = jnp.zeros(out_ref.shape[1:], f32)
        count_ref[t] = 0
        return carry

    lax.fori_loop(0, tiles, clear, 0)

    def group(g, carry):
        base = pl.multiple_of(g * 8, 8)
        sources = src_ref[pl.ds(base, 8), :]
        cells = cell_ref[pl.ds(base, 8), :].astype(f32)
        weights = weight_ref[pl.ds(base, 8), :]
        for w in range(4):
            start = pl.multiple_of((g * 4 + w) * width, width)
            window = flux_ref[:, pl.ds(start, width)]
            for half in range(2):
                j = 2 * w + half
                index = jnp.broadcast_to(sources[j : j + 1], (fields, width))
                picked = jnp.take_along_axis(window, index, axis=1)
                t = tile_ref[base + j]
                r = count_ref[t]
                count_ref[t] = r + 1
                slot = r % share
                lead = (r // share) * tiles + t
                at = pl.multiple_of(slot * fields, fields)
                out_ref[lead, pl.ds(at, fields), :] = picked * weights[j : j + 1]
                out_ref[lead, pl.ds(share * fields + slot, 1), :] = cells[j : j + 1]
        return carry

    lax.fori_loop(0, blocks // 8, group, 0)
    for c, part in enumerate(parts):

        def move(t, carry, c=c, part=part):
            part[t] = out_ref[c * tiles + t]
            return carry

        lax.fori_loop(0, tiles, move, 0)


def pack(margin_tile, atm_flux, margin_source, margin_cell, margin_weight, tiles, cap, parts):
    fields = atm_flux.shape[0]
    share = cap // parts
    rows = share * fields + -(-share // 8) * 8
    width = margin_source.shape[1]
    return pl.pallas_call(
        functools.partial(pack_kernel, cap),
        out_shape=[jax.ShapeDtypeStruct((tiles, rows, width), f32)] * parts,
        in_specs=[smem(), vmem(), vmem(), vmem(), vmem()],
        out_specs=[vmem()] * parts,
        scratch_shapes=[
            pltpu.VMEM((parts * tiles, rows, width), f32),
            pltpu.SMEM((tiles,), jnp.int32),
        ],
        compiler_params=pltpu.CompilerParams(vmem_limit_bytes=VMEM_LIMIT),
        cost_estimate=pl.CostEstimate(flops=10_000_000, bytes_accessed=4_000_000, transcendentals=0),
        name="pack",
    )(margin_tile, atm_flux, margin_source, margin_cell, margin_weight)


def scatter_kernel(cap, fields, tile_rows, tile_cols, start, finish, row_ref, in_ref, *rest):
    if finish:
        forcing_ref, baro_ref, acc_ref = rest[-3:]
    else:
        acc_ref = rest[-1]
    owners = in_ref.shape[0]
    width = in_ref.shape[2]
    highs = tile_cols // LANES
    lines = highs * fields
    group = 4 if cap % 4 == 0 else 1

    def clear(y, carry):
        at = pl.ds(pl.multiple_of(y * lines, lines), lines)
        acc_ref[at, :] = jnp.zeros((lines, LANES), f32) if start else rest[0][at, :]
        return carry

    lax.fori_loop(0, tile_rows, clear, 0)
    low_iota = lax.broadcasted_iota(jnp.int32, (LANES, width), 0)

    def owner_step(o, carry):
        cells = in_ref[o, cap * fields : in_ref.shape[1], :].astype(jnp.int32)
        for g in range(cap // group):
            sums = []
            for r in range(g * group, (g + 1) * group):
                row = row_ref[o * cap + r]
                cols = cells[r : r + 1] - row * tile_cols
                high = jnp.broadcast_to(cols // LANES, (fields, width))
                low = jnp.broadcast_to(cols % LANES, (LANES, width))
                onehot = jnp.where(low_iota == low, 1.0, 0.0).astype(jnp.bfloat16)
                values = in_ref[o, r * fields : (r + 1) * fields, :]
                coarse = values.astype(jnp.bfloat16).astype(f32)
                fine = values - coarse
                picks = [high == h for h in range(highs)]
                left = jnp.concatenate(
                    [jnp.where(p, coarse, 0.0) for p in picks]
                    + [jnp.where(p, fine, 0.0) for p in picks],
                    axis=0,
                ).astype(jnp.bfloat16)
                both = lax.dot_general(
                    left, onehot, (((1,), (1,)), ((), ())), preferred_element_type=f32
                )
                sums.append((row, both[:lines] + both[lines:]))
            for row, part in sums:
                at = pl.ds(pl.multiple_of(row * lines, lines), lines)
                acc_ref[at, :] = acc_ref[at, :] + part
        return carry

    lax.fori_loop(0, owners, owner_step, 0)

    if not finish:
        return

    def unfold(yb, carry):
        ys = pl.ds(pl.multiple_of(yb * 8, 8), 8)
        for h in range(highs):
            cs = slice(h * LANES, (h + 1) * LANES)
            planes = []
            for f in range(fields):
                part = acc_ref[pl.ds(yb * 8 * lines + h * fields + f, 8, stride=lines), :]
                forcing_ref[f, ys, cs] = part
                planes.append(part)
            baro_ref[0, ys, cs] = 0.5 * planes[2]
            baro_ref[1, ys, cs] = 0.5 * planes[0]
            baro_ref[2, ys, cs] = 0.5 * planes[1]
            baro_ref[3, ys, cs] = 0.1 * (planes[6] - planes[5])
        return carry

    lax.fori_loop(0, tile_rows // 8, unfold, 0)


def scatter(rows, arrived, total, cap, fields, tile_rows, tile_cols, finish):
    lines = tile_cols // LANES * fields
    sums = (tile_rows * lines, LANES)
    extra = [] if total is None else [total]
    if finish:
        out_shape = [
            jax.ShapeDtypeStruct((fields, tile_rows, tile_cols), f32),
            jax.ShapeDtypeStruct((4, tile_rows, tile_cols), f32),
        ]
    else:
        out_shape = [jax.ShapeDtypeStruct(sums, f32)]
    return pl.pallas_call(
        functools.partial(
            scatter_kernel, cap, fields, tile_rows, tile_cols, total is None, finish
        ),
        out_shape=out_shape,
        in_specs=[smem(), vmem()] + [vmem()] * len(extra),
        out_specs=[vmem()] * len(out_shape),
        scratch_shapes=[pltpu.VMEM(sums, f32)] if finish else [],
        compiler_params=pltpu.CompilerParams(vmem_limit_bytes=VMEM_LIMIT),
        cost_estimate=pl.CostEstimate(
            flops=2_000_000_000, bytes_accessed=20_000_000, transcendentals=0
        ),
        name="scatter",
    )(rows, arrived, *extra)


def edges_kernel(
    west_ref, east_ref, low_ref, high_ref, mask_west_ref, mask_east_ref,
    first_ref, last_ref, bottom_ref, top_ref,
):
    planes, rows = west_ref.shape[:2]
    lane = lax.broadcasted_iota(jnp.int32, (rows, LANES), 1)
    for src, mask, dst, col in (
        (west_ref, mask_west_ref, first_ref, 0),
        (east_ref, mask_east_ref, last_ref, LANES - 1),
    ):
        total = jnp.zeros((rows, LANES), f32)
        for p in range(planes):
            total = jnp.where(
                lane == p, jnp.broadcast_to(src[p, :, col : col + 1], (rows, LANES)), total
            )
        edge = mask[:, col : col + 1].astype(f32)
        dst[...] = jnp.where(lane == planes, jnp.broadcast_to(edge, (rows, LANES)), total)
    for p in range(planes):
        bottom_ref[p : p + 1, :] = low_ref[p, 0:1, :]
        top_ref[p : p + 1, :] = high_ref[p, 7:8, :]


def tracer_edges(tracers, land_mask):
    planes, rows, cols = tracers.shape
    end = cols // LANES - 1
    top = rows // 8 - 1
    strip = jax.ShapeDtypeStruct((rows, LANES), f32)
    line = jax.ShapeDtypeStruct((planes, cols), f32)
    whole = pl.BlockSpec((rows, LANES), lambda i: (0, 0))
    wide = pl.BlockSpec((planes, cols), lambda i: (0, 0))
    return pl.pallas_call(
        edges_kernel,
        out_shape=(strip, strip, line, line),
        grid=(1,),
        in_specs=[
            pl.BlockSpec((planes, rows, LANES), lambda i: (0, 0, 0)),
            pl.BlockSpec((planes, rows, LANES), lambda i: (0, 0, end)),
            pl.BlockSpec((planes, 8, cols), lambda i: (0, 0, 0)),
            pl.BlockSpec((planes, 8, cols), lambda i: (0, top, 0)),
            pl.BlockSpec((rows, LANES), lambda i: (0, 0)),
            pl.BlockSpec((rows, LANES), lambda i: (0, end)),
        ],
        out_specs=(whole, whole, wide, wide),
        compiler_params=pltpu.CompilerParams(vmem_limit_bytes=VMEM_LIMIT),
        cost_estimate=pl.CostEstimate(flops=1_000_000, bytes_accessed=5_000_000, transcendentals=0),
        name="edges",
    )(tracers, tracers, tracers, tracers, land_mask, land_mask)


WAYS = ((1, 0), (-1, 0), (0, 1), (0, -1), (1, 1), (1, -1), (-1, 1), (-1, -1))


def exchange_kernel(mesh_shape, extras, moving, *refs):
    comps, depth, nx = mesh_shape
    ny = comps * depth
    total = ny * nx
    refs = list(refs)
    if moving:
        outgoing = refs.pop(0)
    band, lines = refs[0], refs[1 : 1 + extras]
    outs = refs[1 + extras : 1 + 2 * extras + len(WAYS)]
    if moving:
        arrived = refs[1 + 2 * extras + len(WAYS)]
        own_sem, out_sems, in_sems = refs[-5:-2]
    send_sems, recv_sems = refs[-2:]
    rows, cols = band.shape[1:]
    c, t, x = [lax.axis_index(axis) for axis in AXES]
    y = c * depth + t
    me = y * nx + x

    def inside(dy, dx):
        return (y + dy >= 0) & (y + dy < ny) & (x + dx >= 0) & (x + dx < nx)

    def place(dy, dx):
        return ((y + dy) // depth, (y + dy) % depth, x + dx)

    def partner(d, sign):
        dt, dc, dx = d % depth, d // depth % comps, d // (depth * comps)
        if sign < 0:
            dt, dc, dx = depth - dt, comps - dc, nx - dx
        return ((c + dc) % comps, (t + dt) % depth, (x + dx) % nx)

    def number(at):
        return (at[0] * depth + at[1]) * nx + at[2]

    def shift(d):
        return pltpu.make_async_remote_copy(
            src_ref=outgoing.at[number(partner(d, 1))],
            dst_ref=arrived.at[me],
            send_sem=out_sems.at[d],
            recv_sem=in_sems.at[d],
            device_id=partner(d, 1),
            device_id_type=pl.DeviceIdType.MESH,
        )

    barrier = pltpu.get_barrier_semaphore()
    if moving:
        own = pltpu.make_async_copy(outgoing.at[me], arrived.at[me], own_sem)
        own.start()

        def greet(d, carry):
            pl.semaphore_signal(
                barrier, inc=1, device_id=partner(d, 1), device_id_type=pl.DeviceIdType.MESH
            )
            return carry

        lax.fori_loop(1, total, greet, 0)
        pl.semaphore_wait(barrier, total - 1)
    else:
        near = jnp.int32(0)
        for way in WAYS:
            near = near + inside(*way).astype(jnp.int32)

            @pl.when(inside(*way))
            def _(way=way):
                pl.semaphore_signal(
                    barrier, inc=1, device_id=place(*way), device_id_type=pl.DeviceIdType.MESH
                )

        pl.semaphore_wait(barrier, near)

    def pieces():
        for k, (dy, dx) in enumerate(WAYS):
            start_y = rows - RIM if dy == 1 else 0
            start_x = cols - LANES if dx == 1 else 0
            tall = RIM if dy else rows
            wide = LANES if dx else cols
            yield (dy, dx), band.at[:, pl.ds(start_y, tall), pl.ds(start_x, wide)]
        for k in range(extras):
            yield WAYS[k], lines[k]

    copies = []
    for k, (way, src) in enumerate(pieces()):
        dst = outs[k]

        def copy(way=way, src=src, dst=dst, k=k):
            return pltpu.make_async_remote_copy(
                src_ref=src,
                dst_ref=dst,
                send_sem=send_sems.at[k],
                recv_sem=recv_sems.at[k],
                device_id=place(*way),
                device_id_type=pl.DeviceIdType.MESH,
            )

        sends, gets = inside(*way), inside(-way[0], -way[1])

        @pl.when(sends)
        def _(copy=copy):
            copy().start()

        @pl.when(jnp.logical_not(gets))
        def _(dst=dst):
            dst[...] = jnp.zeros(dst.shape, f32)

        copies.append((copy, sends, gets))
    if moving:

        def start(d, carry):
            shift(d).start()
            return carry

        lax.fori_loop(1, total, start, 0)
    for copy, sends, gets in copies:

        @pl.when(sends)
        def _(copy=copy):
            copy().wait_send()

        @pl.when(gets)
        def _(copy=copy):
            copy().wait_recv()

    if moving:

        def finish(d, carry):
            shift(d).wait_send()
            came = partner(d, -1)
            pltpu.make_async_remote_copy(
                src_ref=outgoing.at[number(came)],
                dst_ref=arrived.at[number(came)],
                send_sem=out_sems.at[d],
                recv_sem=in_sems.at[d],
                device_id=came,
                device_id_type=pl.DeviceIdType.MESH,
            ).wait_recv()
            return carry

        lax.fori_loop(1, total, finish, 0)
        own.wait()


def exchange(mesh_shape, band, lines, number, outgoing=None):
    count, rows, cols = band.shape
    moving = outgoing is not None
    shapes = [
        (count, RIM if dy else rows, LANES if dx else cols) for dy, dx in WAYS
    ] + [a.shape for a in lines]
    pieces = len(shapes)
    first, sems = [], []
    if moving:
        first = [outgoing]
        shapes.append(outgoing.shape)
        total = outgoing.shape[0]
        sems = [
            pltpu.SemaphoreType.DMA,
            pltpu.SemaphoreType.DMA((total,)),
            pltpu.SemaphoreType.DMA((total,)),
        ]
    return pl.pallas_call(
        functools.partial(exchange_kernel, mesh_shape, len(lines), moving),
        out_shape=[jax.ShapeDtypeStruct(s, f32) for s in shapes],
        in_specs=[vmem()] * (len(first) + 1 + len(lines)),
        out_specs=[vmem()] * len(shapes),
        scratch_shapes=sems
        + [pltpu.SemaphoreType.DMA((pieces,)), pltpu.SemaphoreType.DMA((pieces,))],
        compiler_params=pltpu.CompilerParams(
            collective_id=number, has_side_effects=True, vmem_limit_bytes=VMEM_LIMIT
        ),
        cost_estimate=pl.CostEstimate(flops=1000, bytes_accessed=5_000_000, transcendentals=0),
        name="move" if moving else "exchange",
    )(*first, band, *lines)


def tracer_kernel(
    levels,
    tracer_hbm,
    south_ref,
    north_ref,
    west_ref,
    east_ref,
    mask_south_ref,
    mask_north_ref,
    mask_ref,
    depth_ref,
    flow_ref,
    forcing_ref,
    out_ref,
    held,
    mask_held,
    ratio_ref,
    sems,
):
    planes = held.shape[0]
    rows, cols = mask_ref.shape
    steps = rows // 8
    i = pl.program_id(0)

    def chunk(step):
        at = pl.multiple_of(step * 8, 8)
        return pltpu.make_async_copy(
            tracer_hbm.at[:, pl.ds(at, 8), :], held.at[:, pl.ds(at + 8, 8), :], sems.at[step]
        )

    @pl.when(i == 0)
    def _():
        for s in range(steps):
            chunk(s).start()
        for p in range(planes):
            held[p, 7:8, :] = south_ref[p : p + 1, :]
            held[p, rows + 8 : rows + 9, :] = north_ref[p : p + 1, :]
        mask_held[0:8, :] = mask_south_ref[...]
        mask_held[8 : rows + 8, :] = mask_ref[...].astype(f32)
        mask_held[rows + 8 : rows + 16, :] = mask_north_ref[...]
        chunk(0).wait()

    @pl.when(i < steps - 1)
    def _():
        chunk(i + 1).wait()

    base = pl.multiple_of(i * 8, 8)
    here = pl.ds(base + 8, 8)
    lane = lax.broadcasted_iota(jnp.int32, (8, cols), 1) % LANES
    sub = lax.broadcasted_iota(jnp.int32, (8, cols), 0)
    at_first, at_last = lane == 0, lane == LANES - 1
    at_bottom, at_top = sub == 0, sub == 7
    west_edges = west_ref[pl.ds(base, 8), :]
    east_edges = east_ref[pl.ds(base, 8), :]
    pieces = cols // LANES

    def sides(q, below, above, p):
        parts = [q[:, c * LANES : (c + 1) * LANES] for c in range(pieces)]
        up = [pltpu.roll(a, 1, 1) for a in parts]
        down = [pltpu.roll(a, LANES - 1, 1) for a in parts]
        west_edge = jnp.broadcast_to(west_edges[:, p : p + 1], (8, LANES))
        east_edge = jnp.broadcast_to(east_edges[:, p : p + 1], (8, LANES))
        west = jnp.where(
            at_first, jnp.concatenate([west_edge] + up[:-1], 1), jnp.concatenate(up, 1)
        )
        east = jnp.where(
            at_last, jnp.concatenate(down[1:] + [east_edge], 1), jnp.concatenate(down, 1)
        )
        south = jnp.where(at_bottom, jnp.broadcast_to(below, q.shape), pltpu.roll(q, 1, 0))
        north = jnp.where(at_top, jnp.broadcast_to(above, q.shape), pltpu.roll(q, 7, 0))
        return east, west, north, south

    mask = mask_held[here, :]
    mask_e, mask_w, mask_n, mask_s = sides(
        mask, mask_held[pl.ds(base + 7, 1), :], mask_held[pl.ds(base + 16, 1), :], planes
    )
    inverse = 1.0 / depth_ref[...]
    u = flow_ref[0] * inverse
    v = flow_ref[1] * inverse
    ce = mask_e * (diffuse - advect * jnp.minimum(u, 0.0))
    cw = mask_w * (diffuse + advect * jnp.maximum(u, 0.0))
    cn = mask_n * (diffuse - advect * jnp.minimum(v, 0.0))
    cs = mask_s * (diffuse + advect * jnp.maximum(v, 0.0))
    c0 = 1.0 - (ce + cw + cn + cs)

    depths = np.arange(levels, dtype=np.float32)
    absorb = np.exp(-depths / np.float32(3)) - np.exp(-(depths + 1) / np.float32(3))
    fade = np.exp(-depths / np.float32(2))
    stir = 0.5 * forcing_ref[7] * forcing_ref[7]
    sun = 0.5 * forcing_ref[4]
    ratio = None
    last = [None, None]
    lower = None
    for k in range(levels):
        upper = 0.2 + stir * float(fade[k]) if k < levels - 1 else None
        pivot = 1.0
        if upper is not None:
            pivot = pivot + upper
        if lower is not None:
            pivot = pivot + lower + lower * ratio
        scale = 1.0 / pivot
        if upper is not None:
            ratio = -upper * scale
            ratio_ref[k] = ratio
        for t in range(2):
            p = t * levels + k
            q = held[p, here, :]
            qe, qw, qn, qs = sides(
                q, held[p, pl.ds(base + 7, 1), :], held[p, pl.ds(base + 16, 1), :], p
            )
            side = c0 * q + ce * qe + cw * qw + cn * qn + cs * qs
            if t == 0:
                side = side + sun * float(absorb[k])
                if k == 0:
                    side = side + 0.5 * forcing_ref[3]
            elif k == 0:
                side = side + (0.5 * forcing_ref[5] - 0.3 * forcing_ref[6])
            if lower is not None:
                side = side + lower * last[t]
            last[t] = side * scale
            out_ref[p] = last[t]
        lower = upper
    ocean = mask > 0.5
    for k in range(levels - 1, -1, -1):
        for t in range(2):
            p = t * levels + k
            if k < levels - 1:
                last[t] = out_ref[p] - ratio_ref[k] * last[t]
            out_ref[p] = jnp.where(ocean, last[t], held[p, here, :])


def tracer_step(
    levels, tracers, south, north, west, east, mask_south, mask_north, mask, depth, flow, forcing
):
    planes, rows, cols = tracers.shape

    def band(*lead):
        zeros = (0,) * len(lead)
        return pl.BlockSpec((*lead, 8, cols), lambda i: (*zeros, i, 0))

    def full(a):
        zeros = (0,) * a.ndim
        return pl.BlockSpec(a.shape, lambda i: zeros)

    return pl.pallas_call(
        functools.partial(tracer_kernel, levels),
        out_shape=jax.ShapeDtypeStruct(tracers.shape, f32),
        grid=(rows // 8,),
        in_specs=[
            pl.BlockSpec(memory_space=pl.ANY),
            full(south),
            full(north),
            full(west),
            full(east),
            full(mask_south),
            full(mask_north),
            full(mask),
            band(),
            band(2),
            band(forcing.shape[0]),
        ],
        out_specs=band(planes),
        scratch_shapes=[
            pltpu.VMEM((planes, rows + 16, cols), f32),
            pltpu.VMEM((rows + 16, cols), f32),
            pltpu.VMEM((levels, 8, cols), f32),
            pltpu.SemaphoreType.DMA((rows // 8,)),
        ],
        compiler_params=pltpu.CompilerParams(
            vmem_limit_bytes=VMEM_LIMIT, dimension_semantics=("arbitrary",)
        ),
        cost_estimate=pl.CostEstimate(
            flops=100_000_000, bytes_accessed=40_000_000, transcendentals=0
        ),
        name="tracer",
    )(tracers, south, north, west, east, mask_south, mask_north, mask, depth, flow, forcing)


def baro_kernel(
    height_ref,
    flow_ref,
    mask_ref,
    depth_ref,
    baro_ref,
    *refs,
):
    rows, cols = height_ref.shape
    height_out, flow_out = refs[-2:]

    def widen(k, tile, around):
        s, n, w, e, sw, se, nw, ne = [a[k] for a in around]
        low = jnp.concatenate([sw, s, se], 1)
        mid = jnp.concatenate([w, tile, e], 1)
        top = jnp.concatenate([nw, n, ne], 1)
        return jnp.concatenate([low, mid, top], 0)

    def still(k, tile):
        return widen(k, tile, refs[:8])

    def forced(k):
        return widen(k, baro_ref[k], refs[8:16])

    height = still(0, height_ref[...])
    along = still(1, flow_ref[0])
    across = still(2, flow_ref[1])
    mask = still(3, mask_ref[...].astype(f32))
    bottom = -0.5 * still(4, depth_ref[...])
    pressure, wind_x, wind_y, source = [forced(k) for k in range(4)]
    tall, wide = height.shape

    def slope_x(a):
        return pltpu.roll(a, wide - 1, 1) - pltpu.roll(a, 1, 1)

    def slope_y(a):
        return pltpu.roll(a, tall - 1, 0) - pltpu.roll(a, 1, 0)

    for _ in range(SUB):
        level = mask * (height + pressure)
        along = mask * (damping * along + (bottom * slope_x(level) + wind_x))
        across = mask * (damping * across + (bottom * slope_y(level) + wind_y))
        height = mask * (height - 0.5 * (slope_x(along) + slope_y(across)) + source)
    inner = (slice(RIM, RIM + rows), slice(LANES, LANES + cols))
    height_out[...] = height[inner]
    flow_out[0] = along[inner]
    flow_out[1] = across[inner]


def local(
    mesh_shape,
    atm_flux,
    margin_source,
    margin_cell,
    margin_weight,
    margin_tile,
    land_mask,
    sea_depth,
    sea_height,
    transport,
    tracers,
):
    levels = tracers.shape[1]
    tile_rows, tile_cols = sea_height.shape
    fields = atm_flux.shape[0]
    tiles = mesh_shape[0] * mesh_shape[1] * mesh_shape[2]
    cap = 2 * margin_source.shape[0] // tiles
    parts = 1
    share = cap // parts

    outgoing = pack(
        margin_tile[:, 0], atm_flux, margin_source, margin_cell, margin_weight, tiles, cap, parts
    )

    flat = tracers.reshape(2 * levels, tile_rows, tile_cols)
    still = jnp.stack(
        [sea_height, transport[0], transport[1], land_mask.astype(f32), sea_depth]
    )
    first, last, bottom, top = tracer_edges(flat, land_mask)
    *rim, south, north, west, east, arrived = exchange(
        mesh_shape, still, (top, bottom, last, first), 0, outgoing[0]
    )
    total = None
    for c, arrived in enumerate([arrived]):
        cells = arrived[:, share * fields : share * fields + share, 0]
        slot_rows = cells.astype(jnp.int32) // tile_cols
        done = scatter(
            slot_rows.reshape(-1),
            arrived,
            total,
            share,
            fields,
            tile_rows,
            tile_cols,
            c == parts - 1,
        )
        total = done[0]
    forcing, baro = done
    halo = exchange(mesh_shape, baro, (), 1)
    new_tracers = tracer_step(
        levels,
        flat,
        south,
        north,
        west,
        east,
        rim[0][3],
        rim[1][3],
        land_mask,
        sea_depth,
        transport,
        forcing,
    )
    height, flow = pl.pallas_call(
        baro_kernel,
        out_shape=(
            jax.ShapeDtypeStruct(sea_height.shape, f32),
            jax.ShapeDtypeStruct(transport.shape, f32),
        ),
        in_specs=[vmem()] * (5 + 2 * len(WAYS)),
        out_specs=(vmem(), vmem()),
        compiler_params=pltpu.CompilerParams(vmem_limit_bytes=VMEM_LIMIT),
        cost_estimate=pl.CostEstimate(flops=10_000_000, bytes_accessed=8_000_000, transcendentals=0),
        name="baro",
    )(sea_height, transport, land_mask, sea_depth, baro, *rim, *halo)
    return (height, flow, new_tracers.reshape(tracers.shape))


def solution(mesh):
    in_specs = (
        P(None, AXES),
        P(AXES, None),
        P(AXES, None),
        P(AXES, None),
        P(AXES, None),
        P(("comp", "ty"), "tx"),
        P(("comp", "ty"), "tx"),
        P(("comp", "ty"), "tx"),
        P(None, ("comp", "ty"), "tx"),
        P(None, None, ("comp", "ty"), "tx"),
    )
    out_specs = (
        P(("comp", "ty"), "tx"),
        P(None, ("comp", "ty"), "tx"),
        P(None, None, ("comp", "ty"), "tx"),
    )
    body = functools.partial(local, tuple(mesh.shape[axis] for axis in AXES))
    return jax.shard_map(body, mesh=mesh, in_specs=in_specs, out_specs=out_specs, check_vma=False)
```

```python
import functools

import jax
import jax.numpy as jnp
import numpy as np
from jax import lax
from jax.experimental import pallas as pl
from jax.experimental.pallas import tpu as pltpu
from jax.sharding import PartitionSpec as P

SUB = 3
RIM = 8
LANES = 128
AXES = ("comp", "ty", "tx")

damping = 0.95
advect = 0.15
diffuse = 0.1

f32 = jnp.float32
VMEM_LIMIT = 56 * 1024 * 1024


def vmem():
    return pl.BlockSpec(memory_space=pltpu.VMEM)


def smem():
    return pl.BlockSpec(memory_space=pltpu.SMEM)


def pack_kernel(cap, tile_ref, flux_ref, src_ref, cell_ref, weight_ref, *rest):
    *parts, out_ref, count_ref = rest
    tiles = parts[0].shape[0]
    share = cap // len(parts)
    blocks = src_ref.shape[0]
    fields = flux_ref.shape[0]
    width = src_ref.shape[1]

    def clear(t, carry):
        for c in range(len(parts)):
            out_ref[c * tiles + t] = jnp.zeros(out_ref.shape[1:], f32)
        count_ref[t] = 0
        return carry

    lax.fori_loop(0, tiles, clear, 0)

    def group(g, carry):
        base = pl.multiple_of(g * 8, 8)
        sources = src_ref[pl.ds(base, 8), :]
        cells = cell_ref[pl.ds(base, 8), :].astype(f32)
        weights = weight_ref[pl.ds(base, 8), :]
        for w in range(4):
            start = pl.multiple_of((g * 4 + w) * width, width)
            window = flux_ref[:, pl.ds(start, width)]
            for half in range(2):
                j = 2 * w + half
                index = jnp.broadcast_to(sources[j : j + 1], (fields, width))
                picked = jnp.take_along_axis(window, index, axis=1)
                t = tile_ref[base + j]
                r = count_ref[t]
                count_ref[t] = r + 1
                slot = r % share
                lead = (r // share) * tiles + t
                at = pl.multiple_of(slot * fields, fields)
                out_ref[lead, pl.ds(at, fields), :] = picked * weights[j : j + 1]
                out_ref[lead, pl.ds(share * fields + slot, 1), :] = cells[j : j + 1]
        return carry

    lax.fori_loop(0, blocks // 8, group, 0)
    for c, part in enumerate(parts):

        def move(t, carry, c=c, part=part):
            part[t] = out_ref[c * tiles + t]
            return carry

        lax.fori_loop(0, tiles, move, 0)


def pack(margin_tile, atm_flux, margin_source, margin_cell, margin_weight, tiles, cap, parts):
    fields = atm_flux.shape[0]
    share = cap // parts
    rows = share * fields + -(-share // 8) * 8
    width = margin_source.shape[1]
    return pl.pallas_call(
        functools.partial(pack_kernel, cap),
        out_shape=[jax.ShapeDtypeStruct((tiles, rows, width), f32)] * parts,
        in_specs=[smem(), vmem(), vmem(), vmem(), vmem()],
        out_specs=[vmem()] * parts,
        scratch_shapes=[
            pltpu.VMEM((parts * tiles, rows, width), f32),
            pltpu.SMEM((tiles,), jnp.int32),
        ],
        compiler_params=pltpu.CompilerParams(vmem_limit_bytes=VMEM_LIMIT),
        cost_estimate=pl.CostEstimate(flops=10_000_000, bytes_accessed=4_000_000, transcendentals=0),
        name="pack",
    )(margin_tile, atm_flux, margin_source, margin_cell, margin_weight)


WAYS = ((1, 0), (-1, 0), (0, 1), (0, -1), (1, 1), (1, -1), (-1, 1), (-1, -1))


class Grid:
    def __init__(self, mesh_shape):
        self.comps, self.depth, self.nx = mesh_shape
        self.ny = self.comps * self.depth
        self.total = self.ny * self.nx
        self.c, self.t, self.x = [lax.axis_index(axis) for axis in AXES]
        self.y = self.c * self.depth + self.t

    def inside(self, dy, dx):
        y, x = self.y + dy, self.x + dx
        return (y >= 0) & (y < self.ny) & (x >= 0) & (x < self.nx)

    def place(self, dy, dx):
        return ((self.y + dy) // self.depth, (self.y + dy) % self.depth, self.x + dx)

    def partner(self, d, sign):
        dt, dc = d % self.depth, d // self.depth % self.comps
        dx = d // (self.depth * self.comps)
        if sign < 0:
            dt, dc, dx = self.depth - dt, self.comps - dc, self.nx - dx
        return (
            (self.c + dc) % self.comps,
            (self.t + dt) % self.depth,
            (self.x + dx) % self.nx,
        )

    def number(self, at):
        return (at[0] * self.depth + at[1]) * self.nx + at[2]


def greet_near(grid):
    barrier = pltpu.get_barrier_semaphore()
    near = jnp.int32(0)
    for way in WAYS:
        near = near + grid.inside(*way).astype(jnp.int32)

        @pl.when(grid.inside(*way))
        def _(way=way):
            pl.semaphore_signal(
                barrier, inc=1, device_id=grid.place(*way), device_id_type=pl.DeviceIdType.MESH
            )

    pl.semaphore_wait(barrier, near)


class Halo:
    def __init__(self, grid, band, lines, outs, send_sems, recv_sems):
        rows, cols = band.shape[1:]
        self.copies = []
        for k in range(len(WAYS) + len(lines)):
            way = WAYS[k % len(WAYS)]
            if k < len(WAYS):
                dy, dx = way
                ys = pl.ds(rows - RIM if dy == 1 else 0, RIM if dy else rows)
                xs = pl.ds(cols - LANES if dx == 1 else 0, LANES if dx else cols)
                src = band.at[:, ys, xs]
            else:
                src = lines[k - len(WAYS)]

            def copy(way=way, src=src, k=k):
                return pltpu.make_async_remote_copy(
                    src_ref=src,
                    dst_ref=outs[k],
                    send_sem=send_sems.at[k],
                    recv_sem=recv_sems.at[k],
                    device_id=grid.place(*way),
                    device_id_type=pl.DeviceIdType.MESH,
                )

            gets = grid.inside(-way[0], -way[1])
            self.copies.append((copy, outs[k], grid.inside(*way), gets))

    def start(self):
        for copy, dst, sends, gets in self.copies:

            @pl.when(sends)
            def _(copy=copy):
                copy().start()

            @pl.when(jnp.logical_not(gets))
            def _(dst=dst):
                dst[...] = jnp.zeros(dst.shape, f32)

    def wait(self):
        for copy, _, sends, gets in self.copies:

            @pl.when(sends)
            def _(copy=copy):
                copy().wait_send()

            @pl.when(gets)
            def _(copy=copy):
                copy().wait_recv()


def halo_shapes(count, rows, cols):
    return [(count, RIM if dy else rows, LANES if dx else cols) for dy, dx in WAYS]


def move_kernel(
    mesh_shape,
    cap,
    outgoing,
    tracer_hbm,
    mask_ref,
    height_ref,
    flow_ref,
    depth_ref,
    *refs,
):
    grid = Grid(mesh_shape)
    count = len(WAYS) + 4
    outs = refs[:count]
    forcing_ref, baro_ref = refs[count : count + 2]
    (
        arrived,
        band,
        west_blk,
        east_blk,
        low_blk,
        high_blk,
        top,
        bottom,
        last,
        first,
        spread,
        row_ref,
        own_sem,
        load_sems,
        out_sems,
        in_sems,
        send_sems,
        recv_sems,
    ) = refs[count + 2 :]
    fields, rows, cols = forcing_ref.shape
    planes = west_blk.shape[0]
    width = arrived.shape[2]
    highs = cols // LANES
    lines = highs * fields
    slots = row_ref.shape[0]
    owners = slots // cap
    total = grid.total
    me = grid.number((grid.c, grid.t, grid.x))

    def shift(d):
        to = grid.partner(d, 1)
        return pltpu.make_async_remote_copy(
            src_ref=outgoing.at[grid.number(to)],
            dst_ref=arrived.at[me],
            send_sem=out_sems.at[d],
            recv_sem=in_sems.at[d],
            device_id=to,
            device_id_type=pl.DeviceIdType.MESH,
        )

    own = pltpu.make_async_copy(outgoing.at[me], arrived.at[me], own_sem)
    own.start()
    loads = [
        pltpu.make_async_copy(src, dst, load_sems.at[k])
        for k, (src, dst) in enumerate(
            (
                (tracer_hbm.at[:, :, pl.ds(0, LANES)], west_blk),
                (tracer_hbm.at[:, :, pl.ds(cols - LANES, LANES)], east_blk),
                (tracer_hbm.at[:, pl.ds(0, 8), :], low_blk),
                (tracer_hbm.at[:, pl.ds(rows - 8, 8), :], high_blk),
            )
        )
    ]
    for load in loads:
        load.start()

    barrier = pltpu.get_barrier_semaphore()

    def greet(d, carry):
        pl.semaphore_signal(
            barrier, inc=1, device_id=grid.partner(d, 1), device_id_type=pl.DeviceIdType.MESH
        )
        return carry

    lax.fori_loop(1, total, greet, 0)
    pl.semaphore_wait(barrier, total - 1)

    def start(d, carry):
        shift(d).start()
        return carry

    lax.fori_loop(1, total, start, 0)

    band[0] = height_ref[...]
    band[1] = flow_ref[0]
    band[2] = flow_ref[1]
    band[3] = mask_ref[...].astype(f32)
    band[4] = depth_ref[...]
    for load in loads:
        load.wait()
    lane = lax.broadcasted_iota(jnp.int32, (rows, LANES), 1)
    for src, dst, col, side in (
        (west_blk, first, 0, 0),
        (east_blk, last, LANES - 1, cols - LANES),
    ):
        edge = band[3, :, side : side + LANES][:, col : col + 1]
        values = jnp.where(lane == planes, jnp.broadcast_to(edge, (rows, LANES)), 0.0)
        for p in range(planes):
            column = src[p, :, col : col + 1]
            values = jnp.where(lane == p, jnp.broadcast_to(column, (rows, LANES)), values)
        dst[...] = values
    for p in range(planes):
        bottom[p : p + 1, :] = low_blk[p, 0:1, :]
        top[p : p + 1, :] = high_blk[p, 7:8, :]
    halo = Halo(grid, band, (top, bottom, last, first), outs, send_sems, recv_sems)
    halo.start()

    forcing_ref[...] = jnp.zeros(forcing_ref.shape, f32)
    low_iota = lax.broadcasted_iota(jnp.int32, (LANES, width), 0)
    lane_iota = lax.broadcasted_iota(jnp.int32, (1, LANES), 1)
    unroll = 4 if cap % 4 == 0 else 1

    def group_step(g, carry):
        def owner_step(n, carry):
            d = g * owners + n
            came = grid.partner(d, -1)
            source = grid.number(came)

            @pl.when(d == 0)
            def _():
                own.wait()

            @pl.when(d > 0)
            def _():
                pltpu.make_async_remote_copy(
                    src_ref=outgoing.at[source],
                    dst_ref=arrived.at[source],
                    send_sem=out_sems.at[d],
                    recv_sem=in_sems.at[d],
                    device_id=came,
                    device_id_type=pl.DeviceIdType.MESH,
                ).wait_recv()

            def slot_step(rb, carry):
                for ru in range(unroll):
                    r = rb * unroll + ru
                    cell = arrived[source, pl.ds(cap * fields + r, 1), :].astype(jnp.int32)
                    row = lax.div(cell, jnp.full_like(cell, cols))
                    col = cell - row * cols
                    high = jnp.broadcast_to(col // LANES, (fields, width))
                    low = jnp.broadcast_to(col % LANES, (LANES, width))
                    onehot = jnp.where(low_iota == low, 1.0, 0.0).astype(jnp.bfloat16)
                    at = pl.multiple_of(r * fields, fields)
                    values = arrived[source, pl.ds(at, fields), :]
                    coarse = values.astype(jnp.bfloat16).astype(f32)
                    fine = values - coarse
                    picks = [high == h for h in range(highs)]
                    left = jnp.concatenate(
                        [jnp.where(p, coarse, 0.0) for p in picks]
                        + [jnp.where(p, fine, 0.0) for p in picks],
                        axis=0,
                    ).astype(jnp.bfloat16)
                    both = lax.dot_general(
                        left, onehot, (((1,), (1,)), ((), ())), preferred_element_type=f32
                    )
                    slot = n * cap + r
                    spread[pl.ds(slot, lines, stride=slots), :] = both[:lines] + both[lines:]
                    hit = jnp.broadcast_to(row[:, 0:1], (1, LANES)) == lane_iota
                    row_ref[pl.ds(slot, 1), :] = jnp.where(hit, 1.0, 0.0)
                return carry

            lax.fori_loop(0, cap // unroll, slot_step, 0)
            return carry

        lax.fori_loop(0, owners, owner_step, 0)
        onto = row_ref[...].T[:rows].astype(jnp.bfloat16)

        def field_step(f, carry):
            for h in range(highs):
                base = pl.multiple_of((h * fields + f) * slots, slots)
                values = spread[pl.ds(base, slots), :]
                coarse = values.astype(jnp.bfloat16)
                fine = (values - coarse.astype(f32)).astype(jnp.bfloat16)
                part = jnp.dot(onto, coarse, preferred_element_type=f32)
                part = part + jnp.dot(onto, fine, preferred_element_type=f32)
                cs = slice(h * LANES, (h + 1) * LANES)
                forcing_ref[f, :, cs] = forcing_ref[f, :, cs] + part
            return carry

        lax.fori_loop(0, fields, field_step, 0)
        return carry

    lax.fori_loop(0, total // owners, group_step, 0)
    baro_ref[0] = 0.5 * forcing_ref[2]
    baro_ref[1] = 0.5 * forcing_ref[0]
    baro_ref[2] = 0.5 * forcing_ref[1]
    baro_ref[3] = 0.1 * (forcing_ref[6] - forcing_ref[5])

    halo.wait()

    def finish(d, carry):
        shift(d).wait_send()
        return carry

    lax.fori_loop(1, total, finish, 0)


def move(mesh_shape, cap, fields, outgoing, tracers, mask, height, flow, depth):
    planes, rows, cols = tracers.shape
    total = outgoing.shape[0]
    slots = cap * max(1, min(total, 128 // cap))
    rims = halo_shapes(5, rows, cols)
    lines = [(planes, cols), (planes, cols), (rows, LANES), (rows, LANES)]
    outs = rims + lines + [(fields, rows, cols), (4, rows, cols)]
    pieces = len(rims) + len(lines)
    scratch = (
        [outgoing.shape, (5, rows, cols)]
        + [(planes, rows, LANES)] * 2
        + [(planes, 8, cols)] * 2
        + lines
        + [(cols // LANES * fields * slots, LANES), (slots, LANES)]
    )
    dma = pltpu.SemaphoreType.DMA
    return pl.pallas_call(
        functools.partial(move_kernel, mesh_shape, cap),
        out_shape=[jax.ShapeDtypeStruct(s, f32) for s in outs],
        in_specs=[vmem(), pl.BlockSpec(memory_space=pl.ANY)] + [vmem()] * 4,
        out_specs=[vmem()] * len(outs),
        scratch_shapes=[pltpu.VMEM(s, f32) for s in scratch]
        + [dma, dma((4,)), dma((total,)), dma((total,)), dma((pieces,)), dma((pieces,))],
        compiler_params=pltpu.CompilerParams(
            collective_id=0, has_side_effects=True, vmem_limit_bytes=VMEM_LIMIT
        ),
        cost_estimate=pl.CostEstimate(
            flops=4_000_000_000, bytes_accessed=20_000_000, transcendentals=0
        ),
        name="move",
    )(outgoing, tracers, mask, height, flow, depth)


def exchange_kernel(mesh_shape, band, *refs):
    grid = Grid(mesh_shape)
    greet_near(grid)
    halo = Halo(grid, band, (), refs[:-2], *refs[-2:])
    halo.start()
    halo.wait()


def exchange(mesh_shape, band):
    shapes = halo_shapes(*band.shape)
    dma = pltpu.SemaphoreType.DMA
    return pl.pallas_call(
        functools.partial(exchange_kernel, mesh_shape),
        out_shape=[jax.ShapeDtypeStruct(s, f32) for s in shapes],
        in_specs=[vmem()],
        out_specs=[vmem()] * len(shapes),
        scratch_shapes=[dma((len(shapes),)), dma((len(shapes),))],
        compiler_params=pltpu.CompilerParams(
            collective_id=1, has_side_effects=True, vmem_limit_bytes=VMEM_LIMIT
        ),
        cost_estimate=pl.CostEstimate(flops=1000, bytes_accessed=5_000_000, transcendentals=0),
        name="exchange",
    )(band)


def tracer_kernel(
    levels,
    tracer_hbm,
    south_ref,
    north_ref,
    west_ref,
    east_ref,
    mask_south_ref,
    mask_north_ref,
    mask_ref,
    depth_ref,
    flow_ref,
    forcing_ref,
    out_ref,
    held,
    mask_held,
    ratio_ref,
    sems,
):
    planes = held.shape[0]
    rows, cols = mask_ref.shape
    steps = rows // 8
    i = pl.program_id(0)

    def chunk(step):
        at = pl.multiple_of(step * 8, 8)
        return pltpu.make_async_copy(
            tracer_hbm.at[:, pl.ds(at, 8), :], held.at[:, pl.ds(at + 8, 8), :], sems.at[step]
        )

    @pl.when(i == 0)
    def _():
        for s in range(steps):
            chunk(s).start()
        for p in range(planes):
            held[p, 7:8, :] = south_ref[p : p + 1, :]
            held[p, rows + 8 : rows + 9, :] = north_ref[p : p + 1, :]
        mask_held[0:8, :] = mask_south_ref[3]
        mask_held[8 : rows + 8, :] = mask_ref[...].astype(f32)
        mask_held[rows + 8 : rows + 16, :] = mask_north_ref[3]
        chunk(0).wait()

    @pl.when(i < steps - 1)
    def _():
        chunk(i + 1).wait()

    base = pl.multiple_of(i * 8, 8)
    here = pl.ds(base + 8, 8)
    lane = lax.broadcasted_iota(jnp.int32, (8, cols), 1) % LANES
    sub = lax.broadcasted_iota(jnp.int32, (8, cols), 0)
    at_first, at_last = lane == 0, lane == LANES - 1
    at_bottom, at_top = sub == 0, sub == 7
    west_edges = west_ref[pl.ds(base, 8), :]
    east_edges = east_ref[pl.ds(base, 8), :]
    pieces = cols // LANES

    def sides(q, below, above, p):
        parts = [q[:, c * LANES : (c + 1) * LANES] for c in range(pieces)]
        up = [pltpu.roll(a, 1, 1) for a in parts]
        down = [pltpu.roll(a, LANES - 1, 1) for a in parts]
        west_edge = jnp.broadcast_to(west_edges[:, p : p + 1], (8, LANES))
        east_edge = jnp.broadcast_to(east_edges[:, p : p + 1], (8, LANES))
        west = jnp.where(
            at_first, jnp.concatenate([west_edge] + up[:-1], 1), jnp.concatenate(up, 1)
        )
        east = jnp.where(
            at_last, jnp.concatenate(down[1:] + [east_edge], 1), jnp.concatenate(down, 1)
        )
        south = jnp.where(at_bottom, jnp.broadcast_to(below, q.shape), pltpu.roll(q, 1, 0))
        north = jnp.where(at_top, jnp.broadcast_to(above, q.shape), pltpu.roll(q, 7, 0))
        return east, west, north, south

    mask = mask_held[here, :]
    mask_e, mask_w, mask_n, mask_s = sides(
        mask, mask_held[pl.ds(base + 7, 1), :], mask_held[pl.ds(base + 16, 1), :], planes
    )
    inverse = 1.0 / depth_ref[...]
    u = flow_ref[0] * inverse
    v = flow_ref[1] * inverse
    ce = mask_e * (diffuse - advect * jnp.minimum(u, 0.0))
    cw = mask_w * (diffuse + advect * jnp.maximum(u, 0.0))
    cn = mask_n * (diffuse - advect * jnp.minimum(v, 0.0))
    cs = mask_s * (diffuse + advect * jnp.maximum(v, 0.0))
    c0 = 1.0 - (ce + cw + cn + cs)

    depths = np.arange(levels, dtype=np.float32)
    absorb = np.exp(-depths / np.float32(3)) - np.exp(-(depths + 1) / np.float32(3))
    fade = np.exp(-depths / np.float32(2))
    stir = 0.5 * forcing_ref[7] * forcing_ref[7]
    sun = 0.5 * forcing_ref[4]
    ratio = None
    last = [None, None]
    lower = None
    for k in range(levels):
        upper = 0.2 + stir * float(fade[k]) if k < levels - 1 else None
        pivot = 1.0
        if upper is not None:
            pivot = pivot + upper
        if lower is not None:
            pivot = pivot + lower + lower * ratio
        scale = 1.0 / pivot
        if upper is not None:
            ratio = -upper * scale
            ratio_ref[k] = ratio
        for t in range(2):
            p = t * levels + k
            q = held[p, here, :]
            qe, qw, qn, qs = sides(
                q, held[p, pl.ds(base + 7, 1), :], held[p, pl.ds(base + 16, 1), :], p
            )
            side = c0 * q + ce * qe + cw * qw + cn * qn + cs * qs
            if t == 0:
                side = side + sun * float(absorb[k])
                if k == 0:
                    side = side + 0.5 * forcing_ref[3]
            elif k == 0:
                side = side + (0.5 * forcing_ref[5] - 0.3 * forcing_ref[6])
            if lower is not None:
                side = side + lower * last[t]
            last[t] = side * scale
            out_ref[p] = last[t]
        lower = upper
    ocean = mask > 0.5
    for k in range(levels - 1, -1, -1):
        for t in range(2):
            p = t * levels + k
            if k < levels - 1:
                last[t] = out_ref[p] - ratio_ref[k] * last[t]
            out_ref[p] = jnp.where(ocean, last[t], held[p, here, :])


def tracer_step(
    levels, tracers, south, north, west, east, mask_south, mask_north, mask, depth, flow, forcing
):
    planes, rows, cols = tracers.shape

    def band(*lead):
        zeros = (0,) * len(lead)
        return pl.BlockSpec((*lead, 8, cols), lambda i: (*zeros, i, 0))

    def full(a):
        zeros = (0,) * a.ndim
        return pl.BlockSpec(a.shape, lambda i: zeros)

    return pl.pallas_call(
        functools.partial(tracer_kernel, levels),
        out_shape=jax.ShapeDtypeStruct(tracers.shape, f32),
        grid=(rows // 8,),
        in_specs=[
            pl.BlockSpec(memory_space=pl.ANY),
            full(south),
            full(north),
            full(west),
            full(east),
            full(mask_south),
            full(mask_north),
            full(mask),
            band(),
            band(2),
            band(forcing.shape[0]),
        ],
        out_specs=band(planes),
        scratch_shapes=[
            pltpu.VMEM((planes, rows + 16, cols), f32),
            pltpu.VMEM((rows + 16, cols), f32),
            pltpu.VMEM((levels, 8, cols), f32),
            pltpu.SemaphoreType.DMA((rows // 8,)),
        ],
        compiler_params=pltpu.CompilerParams(
            vmem_limit_bytes=VMEM_LIMIT, dimension_semantics=("arbitrary",)
        ),
        cost_estimate=pl.CostEstimate(
            flops=100_000_000, bytes_accessed=40_000_000, transcendentals=0
        ),
        name="tracer",
    )(tracers, south, north, west, east, mask_south, mask_north, mask, depth, flow, forcing)


def baro_kernel(
    height_ref,
    flow_ref,
    mask_ref,
    depth_ref,
    baro_ref,
    *refs,
):
    rows, cols = height_ref.shape
    height_out, flow_out = refs[-2:]

    def widen(k, tile, around):
        s, n, w, e, sw, se, nw, ne = [a[k] for a in around]
        low = jnp.concatenate([sw, s, se], 1)
        mid = jnp.concatenate([w, tile, e], 1)
        top = jnp.concatenate([nw, n, ne], 1)
        return jnp.concatenate([low, mid, top], 0)

    def still(k, tile):
        return widen(k, tile, refs[:8])

    def forced(k):
        return widen(k, baro_ref[k], refs[8:16])

    height = still(0, height_ref[...])
    along = still(1, flow_ref[0])
    across = still(2, flow_ref[1])
    mask = still(3, mask_ref[...].astype(f32))
    bottom = -0.5 * still(4, depth_ref[...])
    pressure, wind_x, wind_y, source = [forced(k) for k in range(4)]
    tall, wide = height.shape

    def slope_x(a):
        return pltpu.roll(a, wide - 1, 1) - pltpu.roll(a, 1, 1)

    def slope_y(a):
        return pltpu.roll(a, tall - 1, 0) - pltpu.roll(a, 1, 0)

    for _ in range(SUB):
        level = mask * (height + pressure)
        along = mask * (damping * along + (bottom * slope_x(level) + wind_x))
        across = mask * (damping * across + (bottom * slope_y(level) + wind_y))
        height = mask * (height - 0.5 * (slope_x(along) + slope_y(across)) + source)
    inner = (slice(RIM, RIM + rows), slice(LANES, LANES + cols))
    height_out[...] = height[inner]
    flow_out[0] = along[inner]
    flow_out[1] = across[inner]


def local(
    mesh_shape,
    atm_flux,
    margin_source,
    margin_cell,
    margin_weight,
    margin_tile,
    land_mask,
    sea_depth,
    sea_height,
    transport,
    tracers,
):
    levels = tracers.shape[1]
    tile_rows, tile_cols = sea_height.shape
    fields = atm_flux.shape[0]
    tiles = mesh_shape[0] * mesh_shape[1] * mesh_shape[2]
    cap = 2 * margin_source.shape[0] // tiles
    parts = 1

    outgoing = pack(
        margin_tile[:, 0], atm_flux, margin_source, margin_cell, margin_weight, tiles, cap, parts
    )

    flat = tracers.reshape(2 * levels, tile_rows, tile_cols)
    *rim, south, north, west, east, forcing, baro = move(
        mesh_shape,
        cap,
        fields,
        outgoing[0],
        flat,
        land_mask,
        sea_height,
        transport,
        sea_depth,
    )
    halo = exchange(mesh_shape, baro)
    new_tracers = tracer_step(
        levels,
        flat,
        south,
        north,
        west,
        east,
        rim[0],
        rim[1],
        land_mask,
        sea_depth,
        transport,
        forcing,
    )
    height, flow = pl.pallas_call(
        baro_kernel,
        out_shape=(
            jax.ShapeDtypeStruct(sea_height.shape, f32),
            jax.ShapeDtypeStruct(transport.shape, f32),
        ),
        in_specs=[vmem()] * (5 + 2 * len(WAYS)),
        out_specs=(vmem(), vmem()),
        compiler_params=pltpu.CompilerParams(vmem_limit_bytes=VMEM_LIMIT),
        cost_estimate=pl.CostEstimate(flops=10_000_000, bytes_accessed=8_000_000, transcendentals=0),
        name="baro",
    )(sea_height, transport, land_mask, sea_depth, baro, *rim, *halo)
    return (height, flow, new_tracers.reshape(tracers.shape))


def solution(mesh):
    in_specs = (
        P(None, AXES),
        P(AXES, None),
        P(AXES, None),
        P(AXES, None),
        P(AXES, None),
        P(("comp", "ty"), "tx"),
        P(("comp", "ty"), "tx"),
        P(("comp", "ty"), "tx"),
        P(None, ("comp", "ty"), "tx"),
        P(None, None, ("comp", "ty"), "tx"),
    )
    out_specs = (
        P(("comp", "ty"), "tx"),
        P(None, ("comp", "ty"), "tx"),
        P(None, None, ("comp", "ty"), "tx"),
    )
    body = functools.partial(local, tuple(mesh.shape[axis] for axis in AXES))
    return jax.shard_map(body, mesh=mesh, in_specs=in_specs, out_specs=out_specs, check_vma=False)
```

```python
import functools

import jax
import jax.numpy as jnp
import numpy as np
from jax import lax
from jax.experimental import pallas as pl
from jax.experimental.pallas import tpu as pltpu
from jax.sharding import PartitionSpec as P

SUB = 3
RIM = 8
LANES = 128
AXES = ("comp", "ty", "tx")

damping = 0.95
advect = 0.15
diffuse = 0.1

f32 = jnp.float32
VMEM_LIMIT = 56 * 1024 * 1024


def vmem():
    return pl.BlockSpec(memory_space=pltpu.VMEM)


def smem():
    return pl.BlockSpec(memory_space=pltpu.SMEM)


def pack_kernel(cap, tile_ref, flux_ref, src_ref, cell_ref, weight_ref, *rest):
    *parts, out_ref, count_ref = rest
    tiles = parts[0].shape[0]
    share = cap // len(parts)
    blocks = src_ref.shape[0]
    fields = flux_ref.shape[0]
    width = src_ref.shape[1]

    def clear(t, carry):
        for c in range(len(parts)):
            out_ref[c * tiles + t] = jnp.zeros(out_ref.shape[1:], f32)
        count_ref[t] = 0
        return carry

    lax.fori_loop(0, tiles, clear, 0)

    def group(g, carry):
        base = pl.multiple_of(g * 8, 8)
        sources = src_ref[pl.ds(base, 8), :]
        cells = cell_ref[pl.ds(base, 8), :].astype(f32)
        weights = weight_ref[pl.ds(base, 8), :]
        for w in range(4):
            start = pl.multiple_of((g * 4 + w) * width, width)
            window = flux_ref[:, pl.ds(start, width)]
            for half in range(2):
                j = 2 * w + half
                index = jnp.broadcast_to(sources[j : j + 1], (fields, width))
                picked = jnp.take_along_axis(window, index, axis=1)
                t = tile_ref[base + j]
                r = count_ref[t]
                count_ref[t] = r + 1
                slot = r % share
                lead = (r // share) * tiles + t
                at = pl.multiple_of(slot * fields, fields)
                out_ref[lead, pl.ds(at, fields), :] = picked * weights[j : j + 1]
                out_ref[lead, pl.ds(share * fields + slot, 1), :] = cells[j : j + 1]
        return carry

    lax.fori_loop(0, blocks // 8, group, 0)
    for c, part in enumerate(parts):

        def move(t, carry, c=c, part=part):
            part[t] = out_ref[c * tiles + t]
            return carry

        lax.fori_loop(0, tiles, move, 0)


def pack(margin_tile, atm_flux, margin_source, margin_cell, margin_weight, tiles, cap, parts):
    fields = atm_flux.shape[0]
    share = cap // parts
    rows = share * fields + -(-share // 8) * 8
    width = margin_source.shape[1]
    return pl.pallas_call(
        functools.partial(pack_kernel, cap),
        out_shape=[jax.ShapeDtypeStruct((tiles, rows, width), f32)] * parts,
        in_specs=[smem(), vmem(), vmem(), vmem(), vmem()],
        out_specs=[vmem()] * parts,
        scratch_shapes=[
            pltpu.VMEM((parts * tiles, rows, width), f32),
            pltpu.SMEM((tiles,), jnp.int32),
        ],
        compiler_params=pltpu.CompilerParams(vmem_limit_bytes=VMEM_LIMIT),
        cost_estimate=pl.CostEstimate(flops=10_000_000, bytes_accessed=4_000_000, transcendentals=0),
        name="pack",
    )(margin_tile, atm_flux, margin_source, margin_cell, margin_weight)


WAYS = ((1, 0), (-1, 0), (0, 1), (0, -1), (1, 1), (1, -1), (-1, 1), (-1, -1))


class Grid:
    def __init__(self, mesh_shape):
        self.comps, self.depth, self.nx = mesh_shape
        self.ny = self.comps * self.depth
        self.total = self.ny * self.nx
        self.c, self.t, self.x = [lax.axis_index(axis) for axis in AXES]
        self.y = self.c * self.depth + self.t

    def inside(self, dy, dx):
        y, x = self.y + dy, self.x + dx
        return (y >= 0) & (y < self.ny) & (x >= 0) & (x < self.nx)

    def place(self, dy, dx):
        return ((self.y + dy) // self.depth, (self.y + dy) % self.depth, self.x + dx)

    def partner(self, d, sign):
        dt, dc = d % self.depth, d // self.depth % self.comps
        dx = d // (self.depth * self.comps)
        if sign < 0:
            dt, dc, dx = self.depth - dt, self.comps - dc, self.nx - dx
        return (
            (self.c + dc) % self.comps,
            (self.t + dt) % self.depth,
            (self.x + dx) % self.nx,
        )

    def number(self, at):
        return (at[0] * self.depth + at[1]) * self.nx + at[2]


class Halo:
    def __init__(self, grid, band, lines, outs, send_sems, recv_sems):
        rows, cols = band.shape[1:]
        self.copies = []
        for k in range(len(WAYS) + len(lines)):
            way = WAYS[k % len(WAYS)]
            if k < len(WAYS):
                dy, dx = way
                ys = pl.ds(rows - RIM if dy == 1 else 0, RIM if dy else rows)
                xs = pl.ds(cols - LANES if dx == 1 else 0, LANES if dx else cols)
                src = band.at[:, ys, xs]
            else:
                src = lines[k - len(WAYS)]

            def copy(way=way, src=src, k=k):
                return pltpu.make_async_remote_copy(
                    src_ref=src,
                    dst_ref=outs[k],
                    send_sem=send_sems.at[k],
                    recv_sem=recv_sems.at[k],
                    device_id=grid.place(*way),
                    device_id_type=pl.DeviceIdType.MESH,
                )

            gets = grid.inside(-way[0], -way[1])
            self.copies.append((copy, outs[k], grid.inside(*way), gets))

    def start(self):
        for copy, dst, sends, gets in self.copies:

            @pl.when(sends)
            def _(copy=copy):
                copy().start()

            @pl.when(jnp.logical_not(gets))
            def _(dst=dst):
                dst[...] = jnp.zeros(dst.shape, f32)

    def wait(self):
        for copy, _, sends, gets in self.copies:

            @pl.when(sends)
            def _(copy=copy):
                copy().wait_send()

            @pl.when(gets)
            def _(copy=copy):
                copy().wait_recv()


def halo_shapes(count, rows, cols):
    return [(count, RIM if dy else rows, LANES if dx else cols) for dy, dx in WAYS]


def advect_band(i, held, mask_held, depth_ref, flow_ref, west_ref, east_ref, moved_ref):
    planes = held.shape[0]
    cols = held.shape[2]
    base = pl.multiple_of(i * 8, 8)
    here = pl.ds(base + 8, 8)
    lane = lax.broadcasted_iota(jnp.int32, (8, cols), 1) % LANES
    sub = lax.broadcasted_iota(jnp.int32, (8, cols), 0)
    at_first, at_last = lane == 0, lane == LANES - 1
    at_bottom, at_top = sub == 0, sub == 7
    west_edges = west_ref[pl.ds(base, 8), :]
    east_edges = east_ref[pl.ds(base, 8), :]
    pieces = cols // LANES

    def sides(q, below, above, p):
        parts = [q[:, c * LANES : (c + 1) * LANES] for c in range(pieces)]
        up = [pltpu.roll(a, 1, 1) for a in parts]
        down = [pltpu.roll(a, LANES - 1, 1) for a in parts]
        west_edge = jnp.broadcast_to(west_edges[:, p : p + 1], (8, LANES))
        east_edge = jnp.broadcast_to(east_edges[:, p : p + 1], (8, LANES))
        west = jnp.where(
            at_first, jnp.concatenate([west_edge] + up[:-1], 1), jnp.concatenate(up, 1)
        )
        east = jnp.where(
            at_last, jnp.concatenate(down[1:] + [east_edge], 1), jnp.concatenate(down, 1)
        )
        south = jnp.where(at_bottom, jnp.broadcast_to(below, q.shape), pltpu.roll(q, 1, 0))
        north = jnp.where(at_top, jnp.broadcast_to(above, q.shape), pltpu.roll(q, 7, 0))
        return east, west, north, south

    mask = mask_held[here, :]
    mask_e, mask_w, mask_n, mask_s = sides(
        mask, mask_held[pl.ds(base + 7, 1), :], mask_held[pl.ds(base + 16, 1), :], planes
    )
    near = pl.ds(base, 8)
    inverse = 1.0 / depth_ref[near, :]
    u = flow_ref[0, near, :] * inverse
    v = flow_ref[1, near, :] * inverse
    ce = mask_e * (diffuse - advect * jnp.minimum(u, 0.0))
    cw = mask_w * (diffuse + advect * jnp.maximum(u, 0.0))
    cn = mask_n * (diffuse - advect * jnp.minimum(v, 0.0))
    cs = mask_s * (diffuse + advect * jnp.maximum(v, 0.0))
    c0 = 1.0 - (ce + cw + cn + cs)

    ocean = mask > 0.5
    for p in range(planes):
        q = held[p, here, :]
        qe, qw, qn, qs = sides(
            q, held[p, pl.ds(base + 7, 1), :], held[p, pl.ds(base + 16, 1), :], p
        )
        moved = c0 * q + ce * qe + cw * qw + cn * qn + cs * qs
        moved_ref[p, near, :] = jnp.where(ocean, moved, q)


def move_kernel(
    mesh_shape,
    cap,
    outgoing,
    tracer_hbm,
    mask_ref,
    height_ref,
    flow_ref,
    depth_ref,
    *refs,
):
    grid = Grid(mesh_shape)
    count = len(WAYS) + 4
    outs = refs[:count]
    forcing_ref, baro_ref, moved_hbm = refs[count : count + 3]
    baro_outs = refs[count + 3 : count + 3 + len(WAYS)]
    (
        arrived,
        band,
        held,
        mask_held,
        moved,
        top,
        bottom,
        last,
        first,
        spread,
        row_ref,
        own_sem,
        load_sems,
        out_sems,
        in_sems,
        send_sems,
        recv_sems,
        late_send_sems,
        late_recv_sems,
        store_sems,
    ) = refs[count + 3 + len(WAYS) :]
    fields, rows, cols = forcing_ref.shape
    planes = held.shape[0]
    bands = rows // 8
    width = arrived.shape[2]
    highs = cols // LANES
    lines = highs * fields
    slots = row_ref.shape[0]
    owners = slots // cap
    total = grid.total
    me = grid.number((grid.c, grid.t, grid.x))

    def shift(d):
        to = grid.partner(d, 1)
        return pltpu.make_async_remote_copy(
            src_ref=outgoing.at[grid.number(to)],
            dst_ref=arrived.at[me],
            send_sem=out_sems.at[d],
            recv_sem=in_sems.at[d],
            device_id=to,
            device_id_type=pl.DeviceIdType.MESH,
        )

    own = pltpu.make_async_copy(outgoing.at[me], arrived.at[me], own_sem)
    own.start()
    loads = [
        pltpu.make_async_copy(
            tracer_hbm.at[:, pl.ds(8 * k, 8), :],
            held.at[:, pl.ds(8 * k + 8, 8), :],
            load_sems.at[k],
        )
        for k in range(bands)
    ]
    for load in loads:
        load.start()

    barrier = pltpu.get_barrier_semaphore()

    def greet(d, carry):
        pl.semaphore_signal(
            barrier, inc=1, device_id=grid.partner(d, 1), device_id_type=pl.DeviceIdType.MESH
        )
        return carry

    lax.fori_loop(1, total, greet, 0)
    pl.semaphore_wait(barrier, total - 1)

    def start(d, carry):
        shift(d).start()
        return carry

    lax.fori_loop(1, total, start, 0)

    band[0] = height_ref[...]
    band[1] = flow_ref[0]
    band[2] = flow_ref[1]
    band[3] = mask_ref[...].astype(f32)
    band[4] = depth_ref[...]
    for load in loads:
        load.wait()
    lane = lax.broadcasted_iota(jnp.int32, (rows, LANES), 1)
    for dst, col, side in ((first, 0, 0), (last, LANES - 1, cols - LANES)):
        edge = band[3, :, side : side + LANES][:, col : col + 1]
        values = jnp.where(lane == planes, jnp.broadcast_to(edge, (rows, LANES)), 0.0)
        for p in range(planes):
            column = held[p, 8 : rows + 8, side : side + LANES][:, col : col + 1]
            values = jnp.where(lane == p, jnp.broadcast_to(column, (rows, LANES)), values)
        dst[...] = values
    for p in range(planes):
        bottom[p : p + 1, :] = held[p, 8:9, :]
        top[p : p + 1, :] = held[p, rows + 7 : rows + 8, :]
    halo = Halo(grid, band, (top, bottom, last, first), outs, send_sems, recv_sems)
    halo.start()

    forcing_ref[...] = jnp.zeros(forcing_ref.shape, f32)
    low_iota = lax.broadcasted_iota(jnp.int32, (LANES, width), 0)
    lane_iota = lax.broadcasted_iota(jnp.int32, (1, LANES), 1)
    unroll = 4 if cap % 4 == 0 else 1

    def group_step(g, carry):
        def owner_step(n, carry):
            d = g * owners + n
            came = grid.partner(d, -1)
            source = grid.number(came)

            @pl.when(d == 0)
            def _():
                own.wait()

            @pl.when(d > 0)
            def _():
                pltpu.make_async_remote_copy(
                    src_ref=outgoing.at[source],
                    dst_ref=arrived.at[source],
                    send_sem=out_sems.at[d],
                    recv_sem=in_sems.at[d],
                    device_id=came,
                    device_id_type=pl.DeviceIdType.MESH,
                ).wait_recv()

            def slot_step(rb, carry):
                for ru in range(unroll):
                    r = rb * unroll + ru
                    cell = arrived[source, pl.ds(cap * fields + r, 1), :].astype(jnp.int32)
                    row = lax.div(cell, jnp.full_like(cell, cols))
                    col = cell - row * cols
                    high = jnp.broadcast_to(col // LANES, (fields, width))
                    low = jnp.broadcast_to(col % LANES, (LANES, width))
                    onehot = jnp.where(low_iota == low, 1.0, 0.0).astype(jnp.bfloat16)
                    at = pl.multiple_of(r * fields, fields)
                    values = arrived[source, pl.ds(at, fields), :]
                    coarse = values.astype(jnp.bfloat16).astype(f32)
                    fine = values - coarse
                    picks = [high == h for h in range(highs)]
                    left = jnp.concatenate(
                        [jnp.where(p, coarse, 0.0) for p in picks]
                        + [jnp.where(p, fine, 0.0) for p in picks],
                        axis=0,
                    ).astype(jnp.bfloat16)
                    both = lax.dot_general(
                        left, onehot, (((1,), (1,)), ((), ())), preferred_element_type=f32
                    )
                    slot = n * cap + r
                    spread[pl.ds(slot, lines, stride=slots), :] = both[:lines] + both[lines:]
                    hit = jnp.broadcast_to(row[:, 0:1], (1, LANES)) == lane_iota
                    row_ref[pl.ds(slot, 1), :] = jnp.where(hit, 1.0, 0.0)
                return carry

            lax.fori_loop(0, cap // unroll, slot_step, 0)
            return carry

        lax.fori_loop(0, owners, owner_step, 0)
        onto = row_ref[...].T[:rows].astype(jnp.bfloat16)

        def field_step(f, carry):
            for h in range(highs):
                base = pl.multiple_of((h * fields + f) * slots, slots)
                values = spread[pl.ds(base, slots), :]
                coarse = values.astype(jnp.bfloat16)
                fine = (values - coarse.astype(f32)).astype(jnp.bfloat16)
                part = jnp.dot(onto, coarse, preferred_element_type=f32)
                part = part + jnp.dot(onto, fine, preferred_element_type=f32)
                cs = slice(h * LANES, (h + 1) * LANES)
                forcing_ref[f, :, cs] = forcing_ref[f, :, cs] + part
            return carry

        lax.fori_loop(0, fields, field_step, 0)
        return carry

    groups = total // owners
    lax.fori_loop(0, groups // 2, group_step, 0)
    halo.wait()
    south_ref, north_ref, west_ref, east_ref = outs[len(WAYS) :]
    for p in range(planes):
        held[p, 7:8, :] = south_ref[p : p + 1, :]
        held[p, rows + 8 : rows + 9, :] = north_ref[p : p + 1, :]
    mask_held[0:8, :] = outs[0][3]
    mask_held[8 : rows + 8, :] = band[3]
    mask_held[rows + 8 : rows + 16, :] = outs[1][3]

    def store(i):
        at = pl.ds(pl.multiple_of(i * 8, 8), 8)
        return pltpu.make_async_copy(
            moved.at[:, at, :], moved_hbm.at[:, at, :], store_sems.at[i]
        )

    def advect_step(i, carry):
        advect_band(i, held, mask_held, depth_ref, flow_ref, west_ref, east_ref, moved)
        store(i).start()
        return carry

    lax.fori_loop(0, bands, advect_step, 0)
    lax.fori_loop(groups // 2, groups, group_step, 0)
    baro_ref[0] = 0.5 * forcing_ref[2]
    baro_ref[1] = 0.5 * forcing_ref[0]
    baro_ref[2] = 0.5 * forcing_ref[1]
    baro_ref[3] = 0.1 * (forcing_ref[6] - forcing_ref[5])

    late = Halo(grid, baro_ref, (), baro_outs, late_send_sems, late_recv_sems)
    late.start()

    def finish(d, carry):
        shift(d).wait_send()
        return carry

    lax.fori_loop(1, total, finish, 0)

    def stored(i, carry):
        store(i).wait()
        return carry

    lax.fori_loop(0, bands, stored, 0)
    late.wait()


def move(mesh_shape, cap, fields, outgoing, tracers, mask, height, flow, depth):
    planes, rows, cols = tracers.shape
    total = outgoing.shape[0]
    slots = cap * max(1, min(total, 128 // cap))
    rims = halo_shapes(5, rows, cols)
    lines = [(planes, cols), (planes, cols), (rows, LANES), (rows, LANES)]
    outs = rims + lines + [(fields, rows, cols), (4, rows, cols), tracers.shape]
    hbm = len(outs) - 1
    outs = outs + halo_shapes(4, rows, cols)
    places = [vmem()] * len(outs)
    places[hbm] = pl.BlockSpec(memory_space=pl.ANY)
    pieces = len(rims) + len(lines)
    scratch = (
        [outgoing.shape, (5, rows, cols)]
        + [(planes, rows + 16, cols), (rows + 16, cols), tracers.shape]
        + lines
        + [(cols // LANES * fields * slots, LANES), (slots, LANES)]
    )
    dma = pltpu.SemaphoreType.DMA
    return pl.pallas_call(
        functools.partial(move_kernel, mesh_shape, cap),
        out_shape=[jax.ShapeDtypeStruct(s, f32) for s in outs],
        in_specs=[vmem(), pl.BlockSpec(memory_space=pl.ANY)] + [vmem()] * 4,
        out_specs=places,
        scratch_shapes=[pltpu.VMEM(s, f32) for s in scratch]
        + [dma, dma((rows // 8,)), dma((total,)), dma((total,)), dma((pieces,)), dma((pieces,))]
        + [dma((len(WAYS),)), dma((len(WAYS),)), dma((rows // 8,))],
        compiler_params=pltpu.CompilerParams(
            collective_id=0, has_side_effects=True, vmem_limit_bytes=VMEM_LIMIT
        ),
        cost_estimate=pl.CostEstimate(
            flops=4_000_000_000, bytes_accessed=40_000_000, transcendentals=0
        ),
        name="move",
    )(outgoing, tracers, mask, height, flow, depth)


def solve_kernel(levels, moved_ref, mask_ref, forcing_ref, out_ref, ratio_ref):
    depths = np.arange(levels, dtype=np.float32)
    absorb = np.exp(-depths / np.float32(3)) - np.exp(-(depths + 1) / np.float32(3))
    fade = np.exp(-depths / np.float32(2))
    ocean = mask_ref[...].astype(f32)
    floor = 0.2 * ocean
    stir = (0.5 * ocean) * forcing_ref[7] * forcing_ref[7]
    sun = (0.5 * ocean) * forcing_ref[4]
    ratio = None
    last = [None, None]
    lower = None
    for k in range(levels):
        upper = floor + stir * float(fade[k]) if k < levels - 1 else None
        pivot = 1.0
        if upper is not None:
            pivot = pivot + upper
        if lower is not None:
            pivot = pivot + lower + lower * ratio
        scale = 1.0 / pivot
        if upper is not None:
            ratio = -upper * scale
            ratio_ref[k] = ratio
        for t in range(2):
            p = t * levels + k
            side = moved_ref[p]
            if t == 0:
                side = side + sun * float(absorb[k])
                if k == 0:
                    side = side + (0.5 * ocean) * forcing_ref[3]
            elif k == 0:
                side = side + ocean * (0.5 * forcing_ref[5] - 0.3 * forcing_ref[6])
            if lower is not None:
                side = side + lower * last[t]
            last[t] = side * scale
            out_ref[p] = last[t]
        lower = upper
    for k in range(levels - 2, -1, -1):
        for t in range(2):
            p = t * levels + k
            last[t] = out_ref[p] - ratio_ref[k] * last[t]
            out_ref[p] = last[t]


def solve_step(levels, moved, mask, forcing):
    planes, rows, cols = moved.shape
    tall = 16 if rows % 16 == 0 else 8

    def band(*lead):
        zeros = (0,) * len(lead)
        return pl.BlockSpec((*lead, tall, cols), lambda i: (*zeros, i, 0))

    return pl.pallas_call(
        functools.partial(solve_kernel, levels),
        out_shape=jax.ShapeDtypeStruct(moved.shape, f32),
        grid=(rows // tall,),
        in_specs=[band(planes), band(), band(forcing.shape[0])],
        out_specs=band(planes),
        scratch_shapes=[pltpu.VMEM((levels, tall, cols), f32)],
        compiler_params=pltpu.CompilerParams(
            vmem_limit_bytes=VMEM_LIMIT, dimension_semantics=("arbitrary",)
        ),
        cost_estimate=pl.CostEstimate(
            flops=30_000_000, bytes_accessed=25_000_000, transcendentals=0
        ),
        name="solve",
    )(moved, mask, forcing)


def baro_kernel(
    height_ref,
    flow_ref,
    mask_ref,
    depth_ref,
    baro_ref,
    *refs,
):
    rows, cols = height_ref.shape
    height_out, flow_out = refs[-2:]

    def widen(k, tile, around):
        s, n, w, e, sw, se, nw, ne = [a[k] for a in around]
        low = jnp.concatenate([sw, s, se], 1)
        mid = jnp.concatenate([w, tile, e], 1)
        top = jnp.concatenate([nw, n, ne], 1)
        return jnp.concatenate([low, mid, top], 0)

    def still(k, tile):
        return widen(k, tile, refs[:8])

    def forced(k):
        return widen(k, baro_ref[k], refs[8:16])

    height = still(0, height_ref[...])
    along = still(1, flow_ref[0])
    across = still(2, flow_ref[1])
    mask = still(3, mask_ref[...].astype(f32))
    bottom = -0.5 * still(4, depth_ref[...])
    pressure, wind_x, wind_y, source = [forced(k) for k in range(4)]
    tall, wide = height.shape

    def slope_x(a):
        return pltpu.roll(a, wide - 1, 1) - pltpu.roll(a, 1, 1)

    def slope_y(a):
        return pltpu.roll(a, tall - 1, 0) - pltpu.roll(a, 1, 0)

    for _ in range(SUB):
        level = mask * (height + pressure)
        along = mask * (damping * along + (bottom * slope_x(level) + wind_x))
        across = mask * (damping * across + (bottom * slope_y(level) + wind_y))
        height = mask * (height - 0.5 * (slope_x(along) + slope_y(across)) + source)
    inner = (slice(RIM, RIM + rows), slice(LANES, LANES + cols))
    height_out[...] = height[inner]
    flow_out[0] = along[inner]
    flow_out[1] = across[inner]


def local(
    mesh_shape,
    atm_flux,
    margin_source,
    margin_cell,
    margin_weight,
    margin_tile,
    land_mask,
    sea_depth,
    sea_height,
    transport,
    tracers,
):
    levels = tracers.shape[1]
    tile_rows, tile_cols = sea_height.shape
    fields = atm_flux.shape[0]
    tiles = mesh_shape[0] * mesh_shape[1] * mesh_shape[2]
    cap = 2 * margin_source.shape[0] // tiles
    parts = 1

    outgoing = pack(
        margin_tile[:, 0], atm_flux, margin_source, margin_cell, margin_weight, tiles, cap, parts
    )

    flat = tracers.reshape(2 * levels, tile_rows, tile_cols)
    found = move(
        mesh_shape,
        cap,
        fields,
        outgoing[0],
        flat,
        land_mask,
        sea_height,
        transport,
        sea_depth,
    )
    ways = len(WAYS)
    rim, halo = found[:ways], found[-ways:]
    forcing, baro, moved = found[-ways - 3 : -ways]
    new_tracers = solve_step(levels, moved, land_mask, forcing)
    height, flow = pl.pallas_call(
        baro_kernel,
        out_shape=(
            jax.ShapeDtypeStruct(sea_height.shape, f32),
            jax.ShapeDtypeStruct(transport.shape, f32),
        ),
        in_specs=[vmem()] * (5 + 2 * len(WAYS)),
        out_specs=(vmem(), vmem()),
        compiler_params=pltpu.CompilerParams(vmem_limit_bytes=VMEM_LIMIT),
        cost_estimate=pl.CostEstimate(flops=10_000_000, bytes_accessed=8_000_000, transcendentals=0),
        name="baro",
    )(sea_height, transport, land_mask, sea_depth, baro, *rim, *halo)
    return (height, flow, new_tracers.reshape(tracers.shape))


def solution(mesh):
    in_specs = (
        P(None, AXES),
        P(AXES, None),
        P(AXES, None),
        P(AXES, None),
        P(AXES, None),
        P(("comp", "ty"), "tx"),
        P(("comp", "ty"), "tx"),
        P(("comp", "ty"), "tx"),
        P(None, ("comp", "ty"), "tx"),
        P(None, None, ("comp", "ty"), "tx"),
    )
    out_specs = (
        P(("comp", "ty"), "tx"),
        P(None, ("comp", "ty"), "tx"),
        P(None, None, ("comp", "ty"), "tx"),
    )
    body = functools.partial(local, tuple(mesh.shape[axis] for axis in AXES))
    return jax.shard_map(body, mesh=mesh, in_specs=in_specs, out_specs=out_specs, check_vma=False)
```

```python
import functools

import jax
import jax.numpy as jnp
import numpy as np
from jax import lax
from jax.experimental import pallas as pl
from jax.experimental.pallas import tpu as pltpu
from jax.sharding import PartitionSpec as P

SUB = 3
RIM = 8
LANES = 128
AXES = ("comp", "ty", "tx")

damping = 0.95
advect = 0.15
diffuse = 0.1

f32 = jnp.float32
VMEM_LIMIT = 56 * 1024 * 1024


def vmem():
    return pl.BlockSpec(memory_space=pltpu.VMEM)


def smem():
    return pl.BlockSpec(memory_space=pltpu.SMEM)


def pack_kernel(cap, tile_ref, flux_ref, src_ref, cell_ref, weight_ref, *rest):
    *parts, out_ref, count_ref = rest
    tiles = parts[0].shape[0]
    share = cap // len(parts)
    blocks = src_ref.shape[0]
    fields = flux_ref.shape[0]
    width = src_ref.shape[1]

    def clear(t, carry):
        for c in range(len(parts)):
            out_ref[c * tiles + t] = jnp.zeros(out_ref.shape[1:], f32)
        count_ref[t] = 0
        return carry

    lax.fori_loop(0, tiles, clear, 0)

    def group(g, carry):
        base = pl.multiple_of(g * 8, 8)
        sources = src_ref[pl.ds(base, 8), :]
        cells = cell_ref[pl.ds(base, 8), :].astype(f32)
        weights = weight_ref[pl.ds(base, 8), :]
        for w in range(4):
            start = pl.multiple_of((g * 4 + w) * width, width)
            window = flux_ref[:, pl.ds(start, width)]
            for half in range(2):
                j = 2 * w + half
                index = jnp.broadcast_to(sources[j : j + 1], (fields, width))
                picked = jnp.take_along_axis(window, index, axis=1)
                t = tile_ref[base + j]
                r = count_ref[t]
                count_ref[t] = r + 1
                slot = r % share
                lead = (r // share) * tiles + t
                at = pl.multiple_of(slot * fields, fields)
                out_ref[lead, pl.ds(at, fields), :] = picked * weights[j : j + 1]
                out_ref[lead, pl.ds(share * fields + slot, 1), :] = cells[j : j + 1]
        return carry

    lax.fori_loop(0, blocks // 8, group, 0)
    for c, part in enumerate(parts):

        def move(t, carry, c=c, part=part):
            part[t] = out_ref[c * tiles + t]
            return carry

        lax.fori_loop(0, tiles, move, 0)


def pack(margin_tile, atm_flux, margin_source, margin_cell, margin_weight, tiles, cap, parts):
    fields = atm_flux.shape[0]
    share = cap // parts
    rows = share * fields + -(-share // 8) * 8
    width = margin_source.shape[1]
    return pl.pallas_call(
        functools.partial(pack_kernel, cap),
        out_shape=[jax.ShapeDtypeStruct((tiles, rows, width), f32)] * parts,
        in_specs=[smem(), vmem(), vmem(), vmem(), vmem()],
        out_specs=[vmem()] * parts,
        scratch_shapes=[
            pltpu.VMEM((parts * tiles, rows, width), f32),
            pltpu.SMEM((tiles,), jnp.int32),
        ],
        compiler_params=pltpu.CompilerParams(vmem_limit_bytes=VMEM_LIMIT),
        cost_estimate=pl.CostEstimate(flops=10_000_000, bytes_accessed=4_000_000, transcendentals=0),
        name="pack",
    )(margin_tile, atm_flux, margin_source, margin_cell, margin_weight)


WAYS = ((1, 0), (-1, 0), (0, 1), (0, -1), (1, 1), (1, -1), (-1, 1), (-1, -1))


class Grid:
    def __init__(self, mesh_shape):
        self.comps, self.depth, self.nx = mesh_shape
        self.ny = self.comps * self.depth
        self.total = self.ny * self.nx
        self.c, self.t, self.x = [lax.axis_index(axis) for axis in AXES]
        self.y = self.c * self.depth + self.t

    def inside(self, dy, dx):
        y, x = self.y + dy, self.x + dx
        return (y >= 0) & (y < self.ny) & (x >= 0) & (x < self.nx)

    def place(self, dy, dx):
        return ((self.y + dy) // self.depth, (self.y + dy) % self.depth, self.x + dx)

    def partner(self, d, sign):
        dt, dc = d % self.depth, d // self.depth % self.comps
        dx = d // (self.depth * self.comps)
        if sign < 0:
            dt, dc, dx = self.depth - dt, self.comps - dc, self.nx - dx
        return (
            (self.c + dc) % self.comps,
            (self.t + dt) % self.depth,
            (self.x + dx) % self.nx,
        )

    def number(self, at):
        return (at[0] * self.depth + at[1]) * self.nx + at[2]


class Halo:
    def __init__(self, grid, band, lines, outs, send_sems, recv_sems):
        rows, cols = band.shape[1:]
        self.copies = []
        for k in range(len(WAYS) + len(lines)):
            way = WAYS[k % len(WAYS)]
            if k < len(WAYS):
                dy, dx = way
                ys = pl.ds(rows - RIM if dy == 1 else 0, RIM if dy else rows)
                xs = pl.ds(cols - LANES if dx == 1 else 0, LANES if dx else cols)
                src = band.at[:, ys, xs]
            else:
                src = lines[k - len(WAYS)]

            def copy(way=way, src=src, k=k):
                return pltpu.make_async_remote_copy(
                    src_ref=src,
                    dst_ref=outs[k],
                    send_sem=send_sems.at[k],
                    recv_sem=recv_sems.at[k],
                    device_id=grid.place(*way),
                    device_id_type=pl.DeviceIdType.MESH,
                )

            gets = grid.inside(-way[0], -way[1])
            self.copies.append((copy, outs[k], grid.inside(*way), gets))

    def start(self):
        for copy, dst, sends, gets in self.copies:

            @pl.when(sends)
            def _(copy=copy):
                copy().start()

            @pl.when(jnp.logical_not(gets))
            def _(dst=dst):
                dst[...] = jnp.zeros(dst.shape, f32)

    def wait(self):
        for copy, _, sends, gets in self.copies:

            @pl.when(sends)
            def _(copy=copy):
                copy().wait_send()

            @pl.when(gets)
            def _(copy=copy):
                copy().wait_recv()


def halo_shapes(count, rows, cols):
    return [(count, RIM if dy else rows, LANES if dx else cols) for dy, dx in WAYS]


def advect_band(i, held, mask_held, depth_ref, flow_ref, west_ref, east_ref, moved_ref):
    planes = held.shape[0]
    cols = held.shape[2]
    base = pl.multiple_of(i * 8, 8)
    here = pl.ds(base + 8, 8)
    lane = lax.broadcasted_iota(jnp.int32, (8, cols), 1) % LANES
    sub = lax.broadcasted_iota(jnp.int32, (8, cols), 0)
    at_first, at_last = lane == 0, lane == LANES - 1
    at_bottom, at_top = sub == 0, sub == 7
    west_edges = west_ref[pl.ds(base, 8), :]
    east_edges = east_ref[pl.ds(base, 8), :]
    pieces = cols // LANES

    def sides(q, below, above, p):
        parts = [q[:, c * LANES : (c + 1) * LANES] for c in range(pieces)]
        up = [pltpu.roll(a, 1, 1) for a in parts]
        down = [pltpu.roll(a, LANES - 1, 1) for a in parts]
        west_edge = jnp.broadcast_to(west_edges[:, p : p + 1], (8, LANES))
        east_edge = jnp.broadcast_to(east_edges[:, p : p + 1], (8, LANES))
        west = jnp.where(
            at_first, jnp.concatenate([west_edge] + up[:-1], 1), jnp.concatenate(up, 1)
        )
        east = jnp.where(
            at_last, jnp.concatenate(down[1:] + [east_edge], 1), jnp.concatenate(down, 1)
        )
        south = jnp.where(at_bottom, jnp.broadcast_to(below, q.shape), pltpu.roll(q, 1, 0))
        north = jnp.where(at_top, jnp.broadcast_to(above, q.shape), pltpu.roll(q, 7, 0))
        return east, west, north, south

    mask = mask_held[here, :]
    mask_e, mask_w, mask_n, mask_s = sides(
        mask, mask_held[pl.ds(base + 7, 1), :], mask_held[pl.ds(base + 16, 1), :], planes
    )
    near = pl.ds(base, 8)
    inverse = 1.0 / depth_ref[near, :]
    u = flow_ref[0, near, :] * inverse
    v = flow_ref[1, near, :] * inverse
    ce = mask_e * (diffuse - advect * jnp.minimum(u, 0.0))
    cw = mask_w * (diffuse + advect * jnp.maximum(u, 0.0))
    cn = mask_n * (diffuse - advect * jnp.minimum(v, 0.0))
    cs = mask_s * (diffuse + advect * jnp.maximum(v, 0.0))
    c0 = 1.0 - (ce + cw + cn + cs)

    ocean = mask > 0.5
    for p in range(planes):
        q = held[p, here, :]
        qe, qw, qn, qs = sides(
            q, held[p, pl.ds(base + 7, 1), :], held[p, pl.ds(base + 16, 1), :], p
        )
        moved = c0 * q + ce * qe + cw * qw + cn * qn + cs * qs
        moved_ref[p, near, :] = jnp.where(ocean, moved, q)


def move_kernel(
    mesh_shape,
    cap,
    outgoing,
    tracer_hbm,
    mask_ref,
    height_ref,
    flow_ref,
    depth_ref,
    *refs,
):
    grid = Grid(mesh_shape)
    count = len(WAYS) + 4
    outs = refs[:count]
    forcing_ref, baro_ref, moved_hbm = refs[count : count + 3]
    baro_outs = refs[count + 3 : count + 3 + len(WAYS)]
    (
        arrived,
        band,
        held,
        mask_held,
        moved,
        top,
        bottom,
        last,
        first,
        spread,
        row_ref,
        own_sem,
        load_sems,
        out_sems,
        in_sems,
        send_sems,
        recv_sems,
        late_send_sems,
        late_recv_sems,
        store_sems,
    ) = refs[count + 3 + len(WAYS) :]
    fields, rows, cols = forcing_ref.shape
    planes = held.shape[0]
    bands = rows // 8
    width = arrived.shape[2]
    highs = cols // LANES
    lines = highs * fields
    slots = row_ref.shape[0]
    owners = slots // cap
    total = grid.total
    me = grid.number((grid.c, grid.t, grid.x))

    def shift(d):
        to = grid.partner(d, 1)
        return pltpu.make_async_remote_copy(
            src_ref=outgoing.at[grid.number(to)],
            dst_ref=arrived.at[me],
            send_sem=out_sems.at[d],
            recv_sem=in_sems.at[d],
            device_id=to,
            device_id_type=pl.DeviceIdType.MESH,
        )

    own = pltpu.make_async_copy(outgoing.at[me], arrived.at[me], own_sem)
    own.start()
    loads = [
        pltpu.make_async_copy(
            tracer_hbm.at[:, pl.ds(8 * k, 8), :],
            held.at[:, pl.ds(8 * k + 8, 8), :],
            load_sems.at[k],
        )
        for k in range(bands)
    ]
    for load in loads:
        load.start()

    barrier = pltpu.get_barrier_semaphore()

    def greet(d, carry):
        pl.semaphore_signal(
            barrier, inc=1, device_id=grid.partner(d, 1), device_id_type=pl.DeviceIdType.MESH
        )
        return carry

    lax.fori_loop(1, total, greet, 0)
    pl.semaphore_wait(barrier, total - 1)

    def start(d, carry):
        shift(d).start()
        return carry

    early = min(total, grid.comps * grid.depth)
    lax.fori_loop(1, early, start, 0)

    band[0] = height_ref[...]
    band[1] = flow_ref[0]
    band[2] = flow_ref[1]
    band[3] = mask_ref[...].astype(f32)
    band[4] = depth_ref[...]
    for load in loads:
        load.wait()
    lane = lax.broadcasted_iota(jnp.int32, (rows, LANES), 1)
    for dst, col, side in ((first, 0, 0), (last, LANES - 1, cols - LANES)):
        edge = band[3, :, side : side + LANES][:, col : col + 1]
        values = jnp.where(lane == planes, jnp.broadcast_to(edge, (rows, LANES)), 0.0)
        for p in range(planes):
            column = held[p, 8 : rows + 8, side : side + LANES][:, col : col + 1]
            values = jnp.where(lane == p, jnp.broadcast_to(column, (rows, LANES)), values)
        dst[...] = values
    for p in range(planes):
        bottom[p : p + 1, :] = held[p, 8:9, :]
        top[p : p + 1, :] = held[p, rows + 7 : rows + 8, :]
    halo = Halo(grid, band, (top, bottom, last, first), outs, send_sems, recv_sems)
    halo.start()
    lax.fori_loop(early, total, start, 0)

    forcing_ref[...] = jnp.zeros(forcing_ref.shape, f32)
    low_iota = lax.broadcasted_iota(jnp.int32, (LANES, width), 0)
    lane_iota = lax.broadcasted_iota(jnp.int32, (1, LANES), 1)
    unroll = 4 if cap % 4 == 0 else 1

    def group_step(g, carry):
        def owner_step(n, carry):
            d = g * owners + n
            came = grid.partner(d, -1)
            source = grid.number(came)

            @pl.when(d == 0)
            def _():
                own.wait()

            @pl.when(d > 0)
            def _():
                pltpu.make_async_remote_copy(
                    src_ref=outgoing.at[source],
                    dst_ref=arrived.at[source],
                    send_sem=out_sems.at[d],
                    recv_sem=in_sems.at[d],
                    device_id=came,
                    device_id_type=pl.DeviceIdType.MESH,
                ).wait_recv()

            def slot_step(rb, carry):
                for ru in range(unroll):
                    r = rb * unroll + ru
                    cell = arrived[source, pl.ds(cap * fields + r, 1), :].astype(jnp.int32)
                    row = lax.div(cell, jnp.full_like(cell, cols))
                    col = cell - row * cols
                    high = jnp.broadcast_to(col // LANES, (fields, width))
                    low = jnp.broadcast_to(col % LANES, (LANES, width))
                    onehot = jnp.where(low_iota == low, 1.0, 0.0).astype(jnp.bfloat16)
                    at = pl.multiple_of(r * fields, fields)
                    values = arrived[source, pl.ds(at, fields), :]
                    coarse = values.astype(jnp.bfloat16).astype(f32)
                    fine = values - coarse
                    picks = [high == h for h in range(highs)]
                    left = jnp.concatenate(
                        [jnp.where(p, coarse, 0.0) for p in picks]
                        + [jnp.where(p, fine, 0.0) for p in picks],
                        axis=0,
                    ).astype(jnp.bfloat16)
                    both = lax.dot_general(
                        left, onehot, (((1,), (1,)), ((), ())), preferred_element_type=f32
                    )
                    slot = n * cap + r
                    spread[pl.ds(slot, lines, stride=slots), :] = both[:lines] + both[lines:]
                    hit = jnp.broadcast_to(row[:, 0:1], (1, LANES)) == lane_iota
                    row_ref[pl.ds(slot, 1), :] = jnp.where(hit, 1.0, 0.0)
                return carry

            lax.fori_loop(0, cap // unroll, slot_step, 0)
            return carry

        lax.fori_loop(0, owners, owner_step, 0)
        onto = row_ref[...].T[:rows].astype(jnp.bfloat16)

        def field_step(f, carry):
            for h in range(highs):
                base = pl.multiple_of((h * fields + f) * slots, slots)
                values = spread[pl.ds(base, slots), :]
                coarse = values.astype(jnp.bfloat16)
                fine = (values - coarse.astype(f32)).astype(jnp.bfloat16)
                part = jnp.dot(onto, coarse, preferred_element_type=f32)
                part = part + jnp.dot(onto, fine, preferred_element_type=f32)
                cs = slice(h * LANES, (h + 1) * LANES)
                forcing_ref[f, :, cs] = forcing_ref[f, :, cs] + part
            return carry

        lax.fori_loop(0, fields, field_step, 0)
        return carry

    groups = total // owners
    lax.fori_loop(0, groups // 2, group_step, 0)
    halo.wait()
    south_ref, north_ref, west_ref, east_ref = outs[len(WAYS) :]
    for p in range(planes):
        held[p, 7:8, :] = south_ref[p : p + 1, :]
        held[p, rows + 8 : rows + 9, :] = north_ref[p : p + 1, :]
    mask_held[0:8, :] = outs[0][3]
    mask_held[8 : rows + 8, :] = band[3]
    mask_held[rows + 8 : rows + 16, :] = outs[1][3]

    def store(i):
        at = pl.ds(pl.multiple_of(i * 8, 8), 8)
        return pltpu.make_async_copy(
            moved.at[:, at, :], moved_hbm.at[:, at, :], store_sems.at[i]
        )

    def advect_step(i, carry):
        advect_band(i, held, mask_held, depth_ref, flow_ref, west_ref, east_ref, moved)
        store(i).start()
        return carry

    lax.fori_loop(0, bands, advect_step, 0)
    lax.fori_loop(groups // 2, groups, group_step, 0)
    baro_ref[0] = 0.5 * forcing_ref[2]
    baro_ref[1] = 0.5 * forcing_ref[0]
    baro_ref[2] = 0.5 * forcing_ref[1]
    baro_ref[3] = 0.1 * (forcing_ref[6] - forcing_ref[5])

    late = Halo(grid, baro_ref, (), baro_outs, late_send_sems, late_recv_sems)
    late.start()

    def finish(d, carry):
        shift(d).wait_send()
        return carry

    lax.fori_loop(1, total, finish, 0)

    def stored(i, carry):
        store(i).wait()
        return carry

    lax.fori_loop(0, bands, stored, 0)
    late.wait()


def move(mesh_shape, cap, fields, outgoing, tracers, mask, height, flow, depth):
    planes, rows, cols = tracers.shape
    total = outgoing.shape[0]
    slots = cap * max(1, min(total, 128 // cap))
    rims = halo_shapes(5, rows, cols)
    lines = [(planes, cols), (planes, cols), (rows, LANES), (rows, LANES)]
    outs = rims + lines + [(fields, rows, cols), (4, rows, cols), tracers.shape]
    hbm = len(outs) - 1
    outs = outs + halo_shapes(4, rows, cols)
    places = [vmem()] * len(outs)
    places[hbm] = pl.BlockSpec(memory_space=pl.ANY)
    pieces = len(rims) + len(lines)
    scratch = (
        [outgoing.shape, (5, rows, cols)]
        + [(planes, rows + 16, cols), (rows + 16, cols), tracers.shape]
        + lines
        + [(cols // LANES * fields * slots, LANES), (slots, LANES)]
    )
    dma = pltpu.SemaphoreType.DMA
    return pl.pallas_call(
        functools.partial(move_kernel, mesh_shape, cap),
        out_shape=[jax.ShapeDtypeStruct(s, f32) for s in outs],
        in_specs=[vmem(), pl.BlockSpec(memory_space=pl.ANY)] + [vmem()] * 4,
        out_specs=places,
        scratch_shapes=[pltpu.VMEM(s, f32) for s in scratch]
        + [dma, dma((rows // 8,)), dma((total,)), dma((total,)), dma((pieces,)), dma((pieces,))]
        + [dma((len(WAYS),)), dma((len(WAYS),)), dma((rows // 8,))],
        compiler_params=pltpu.CompilerParams(
            collective_id=0, has_side_effects=True, vmem_limit_bytes=VMEM_LIMIT
        ),
        cost_estimate=pl.CostEstimate(
            flops=4_000_000_000, bytes_accessed=40_000_000, transcendentals=0
        ),
        name="move",
    )(outgoing, tracers, mask, height, flow, depth)


def solve_kernel(levels, moved_ref, mask_ref, forcing_ref, out_ref, ratio_ref):
    depths = np.arange(levels, dtype=np.float32)
    absorb = np.exp(-depths / np.float32(3)) - np.exp(-(depths + 1) / np.float32(3))
    fade = np.exp(-depths / np.float32(2))
    ocean = mask_ref[...].astype(f32)
    floor = 0.2 * ocean
    stir = (0.5 * ocean) * forcing_ref[7] * forcing_ref[7]
    sun = (0.5 * ocean) * forcing_ref[4]
    ratio = None
    last = [None, None]
    lower = None
    for k in range(levels):
        upper = floor + stir * float(fade[k]) if k < levels - 1 else None
        pivot = 1.0
        if upper is not None:
            pivot = pivot + upper
        if lower is not None:
            pivot = pivot + lower + lower * ratio
        scale = 1.0 / pivot
        if upper is not None:
            ratio = -upper * scale
            ratio_ref[k] = ratio
        for t in range(2):
            p = t * levels + k
            side = moved_ref[p]
            if t == 0:
                side = side + sun * float(absorb[k])
                if k == 0:
                    side = side + (0.5 * ocean) * forcing_ref[3]
            elif k == 0:
                side = side + ocean * (0.5 * forcing_ref[5] - 0.3 * forcing_ref[6])
            if lower is not None:
                side = side + lower * last[t]
            last[t] = side * scale
            out_ref[p] = last[t]
        lower = upper
    for k in range(levels - 2, -1, -1):
        for t in range(2):
            p = t * levels + k
            last[t] = out_ref[p] - ratio_ref[k] * last[t]
            out_ref[p] = last[t]


def solve_step(levels, moved, mask, forcing):
    planes, rows, cols = moved.shape
    tall = 16 if rows % 16 == 0 else 8

    def band(*lead):
        zeros = (0,) * len(lead)
        return pl.BlockSpec((*lead, tall, cols), lambda i: (*zeros, i, 0))

    return pl.pallas_call(
        functools.partial(solve_kernel, levels),
        out_shape=jax.ShapeDtypeStruct(moved.shape, f32),
        grid=(rows // tall,),
        in_specs=[band(planes), band(), band(forcing.shape[0])],
        out_specs=band(planes),
        scratch_shapes=[pltpu.VMEM((levels, tall, cols), f32)],
        compiler_params=pltpu.CompilerParams(
            vmem_limit_bytes=VMEM_LIMIT, dimension_semantics=("arbitrary",)
        ),
        cost_estimate=pl.CostEstimate(
            flops=30_000_000, bytes_accessed=25_000_000, transcendentals=0
        ),
        name="solve",
    )(moved, mask, forcing)


def baro_kernel(
    height_ref,
    flow_ref,
    mask_ref,
    depth_ref,
    baro_ref,
    *refs,
):
    rows, cols = height_ref.shape
    height_out, flow_out = refs[-2:]

    def widen(k, tile, around):
        s, n, w, e, sw, se, nw, ne = [a[k] for a in around]
        low = jnp.concatenate([sw, s, se], 1)
        mid = jnp.concatenate([w, tile, e], 1)
        top = jnp.concatenate([nw, n, ne], 1)
        return jnp.concatenate([low, mid, top], 0)

    def still(k, tile):
        return widen(k, tile, refs[:8])

    def forced(k):
        return widen(k, baro_ref[k], refs[8:16])

    height = still(0, height_ref[...])
    along = still(1, flow_ref[0])
    across = still(2, flow_ref[1])
    mask = still(3, mask_ref[...].astype(f32))
    bottom = -0.5 * still(4, depth_ref[...])
    pressure, wind_x, wind_y, source = [forced(k) for k in range(4)]
    tall, wide = height.shape

    def slope_x(a):
        return pltpu.roll(a, wide - 1, 1) - pltpu.roll(a, 1, 1)

    def slope_y(a):
        return pltpu.roll(a, tall - 1, 0) - pltpu.roll(a, 1, 0)

    for _ in range(SUB):
        level = mask * (height + pressure)
        along = mask * (damping * along + (bottom * slope_x(level) + wind_x))
        across = mask * (damping * across + (bottom * slope_y(level) + wind_y))
        height = mask * (height - 0.5 * (slope_x(along) + slope_y(across)) + source)
    inner = (slice(RIM, RIM + rows), slice(LANES, LANES + cols))
    height_out[...] = height[inner]
    flow_out[0] = along[inner]
    flow_out[1] = across[inner]


def local(
    mesh_shape,
    atm_flux,
    margin_source,
    margin_cell,
    margin_weight,
    margin_tile,
    land_mask,
    sea_depth,
    sea_height,
    transport,
    tracers,
):
    levels = tracers.shape[1]
    tile_rows, tile_cols = sea_height.shape
    fields = atm_flux.shape[0]
    tiles = mesh_shape[0] * mesh_shape[1] * mesh_shape[2]
    cap = 2 * margin_source.shape[0] // tiles
    parts = 1

    outgoing = pack(
        margin_tile[:, 0], atm_flux, margin_source, margin_cell, margin_weight, tiles, cap, parts
    )

    flat = tracers.reshape(2 * levels, tile_rows, tile_cols)
    found = move(
        mesh_shape,
        cap,
        fields,
        outgoing[0],
        flat,
        land_mask,
        sea_height,
        transport,
        sea_depth,
    )
    ways = len(WAYS)
    rim, halo = found[:ways], found[-ways:]
    forcing, baro, moved = found[-ways - 3 : -ways]
    new_tracers = solve_step(levels, moved, land_mask, forcing)
    height, flow = pl.pallas_call(
        baro_kernel,
        out_shape=(
            jax.ShapeDtypeStruct(sea_height.shape, f32),
            jax.ShapeDtypeStruct(transport.shape, f32),
        ),
        in_specs=[vmem()] * (5 + 2 * len(WAYS)),
        out_specs=(vmem(), vmem()),
        compiler_params=pltpu.CompilerParams(vmem_limit_bytes=VMEM_LIMIT),
        cost_estimate=pl.CostEstimate(flops=10_000_000, bytes_accessed=8_000_000, transcendentals=0),
        name="baro",
    )(sea_height, transport, land_mask, sea_depth, baro, *rim, *halo)
    return (height, flow, new_tracers.reshape(tracers.shape))


def solution(mesh):
    in_specs = (
        P(None, AXES),
        P(AXES, None),
        P(AXES, None),
        P(AXES, None),
        P(AXES, None),
        P(("comp", "ty"), "tx"),
        P(("comp", "ty"), "tx"),
        P(("comp", "ty"), "tx"),
        P(None, ("comp", "ty"), "tx"),
        P(None, None, ("comp", "ty"), "tx"),
    )
    out_specs = (
        P(("comp", "ty"), "tx"),
        P(None, ("comp", "ty"), "tx"),
        P(None, None, ("comp", "ty"), "tx"),
    )
    body = functools.partial(local, tuple(mesh.shape[axis] for axis in AXES))
    return jax.shard_map(body, mesh=mesh, in_specs=in_specs, out_specs=out_specs, check_vma=False)
```
